32 devices in a mesh: grp: 4 (over x, core), ep: 8 (over z, y).
Axes of the slice: x: 2, y: 2, z: 4, core: 2. Of those that a mesh axis runs over, the one named last changes fastest.
Arguments:
- tokens: bfloat16 [4, 32, 5120], P('grp', 'ep'), may hold values from -6 to 6
- cotangent: bfloat16 [4, 32, 5120], P('grp', 'ep'), may hold values from -1.5 to 1.5
- counts: int32 [4, 8, 1], P('grp', 'ep'), may hold values from 0 to 4, as said below
- destination: int32 [4, 8, 4], P('grp', 'ep'), may hold values from 0 to 3, each once within a row
- placement: int32 [8], replicated, may hold values from 0 to 7, each once
- gate_up_weight: bfloat16 [8, 2, 5120, 128], P('ep', None, 'grp'), may hold values from -0.078125 to 0.078125
- down_weight: bfloat16 [8, 5120, 128], P('ep', 'grp'), may hold values from -0.1875 to 0.1875
Outputs:
- layer_out: bfloat16 [4, 32, 5120], P('grp', 'ep')
- input_grad: bfloat16 [4, 32, 5120], P('grp', 'ep')
- gate_up_grad: float32 [8, 2, 5120, 128], P('ep', None, 'grp')
- down_grad: float32 [8, 5120, 128], P('ep', 'grp')
The draws below stay inside these ranges and needn't reach their ends.
Inputs may be any that keep to these rules, and one draw needn't show every extreme that they name: counts[g, j, e] is the number of kept slots of expert e on device (g, j) after reassignment; some device has all 4 slots of an expert kept in every draw. `destination`: the 4 blocks of one device go to 4 different groups. `placement`: each expert slice is served by exactly one owner.
All inputs are finite; a program needn't handle non-finite values.
Results may differ from the reference program's by a relative error of at most 0.017.
Values may be sent and summed in bfloat16 or wider, within the bound.
A program may use at most 64 MiB of HBM per device.

```python
import jax
import jax.numpy as jnp
from jax import lax

D = 5120
SLICE = 128
SPLIT = 8
CAP = 4
HID = 1024
EXP_G = 1
TOK_DEV = 4
GROUPS = 4
OWNERS = 8
N_GRP = 4
N_EP = 8


def draw_counts(key, part):
    drawn = jax.random.randint(key, (GROUPS, OWNERS, EXP_G), 0, CAP + 1)
    return drawn.at[0, 0, 0].set(CAP).astype(jnp.int32)


def block_scale(key, dims, shards, smallest, high):
    level, own = 1.0, jax.random.fold_in(key, 6)
    for axis_at, parts in shards:
        heights = jnp.exp(jax.random.uniform(jax.random.fold_in(own, axis_at), (parts,), jnp.float32, smallest / len(shards), high / len(shards)))
        level = level * jnp.repeat(heights, dims[axis_at] // parts).reshape([-1 if axis == axis_at else 1 for axis in range(len(dims))])
    return level


def gaussian(stream_key, dims, scale, bound, cuts=(), kind=jnp.bfloat16):
    values = jax.random.normal(stream_key, dims, jnp.float32) * scale
    if len(cuts) > 0:
        values = block_scale(stream_key, dims, cuts, -0.22, 0.18) * values
    return jnp.clip(values, min=-bound, max=bound).astype(kind)


def setup_inputs(seed: int = 0) -> dict:
    key_list = jax.random.split(jax.random.key(seed), 8)
    tokens = gaussian(key_list[0], (GROUPS, OWNERS * TOK_DEV, D), 1.0, 6.0, ((0, 4), (1, 8)))
    cotangent = gaussian(key_list[1], (GROUPS, OWNERS * TOK_DEV, D), 0.25, 1.5, ((0, 4), (1, 8)))
    counts = draw_counts(jax.random.fold_in(key_list[7], 71), 0)
    destination = jax.vmap(lambda own: jax.random.permutation(own, GROUPS))(jax.random.split(key_list[3], GROUPS * OWNERS)).reshape((GROUPS, OWNERS, GROUPS)).astype(jnp.int32)
    placement = jax.random.permutation(key_list[4], OWNERS).astype(jnp.int32)
    gate_up_weight = gaussian(key_list[5], (OWNERS, 2, D, SLICE), D ** -0.5, 0.078125, ((0, 8), (2, 4)))
    down_weight = gaussian(key_list[6], (OWNERS, D, SLICE), HID ** -0.5, 0.1875, ((0, 8), (1, 4)))
    return dict(tokens=tokens, cotangent=cotangent, counts=counts, destination=destination, placement=placement, gate_up_weight=gate_up_weight, down_weight=down_weight)


def swiglu_backward(gate_up, hidden_grad):
    gate_part = gate_up[0]
    up_part = gate_up[1]
    sigmoid_gate = jax.nn.sigmoid(gate_part)
    activated = gate_part * sigmoid_gate
    hidden = (activated * up_part).astype(jnp.bfloat16)
    gate_grad = hidden_grad * up_part * sigmoid_gate * (1.0 + gate_part * (1.0 - sigmoid_gate))
    up_grad = hidden_grad * activated
    return hidden, jnp.stack([gate_grad, up_grad]).astype(jnp.bfloat16)


def widen(value):
    return lax.optimization_barrier(value).astype(jnp.float32)


def reference(tokens, cotangent, counts, destination, placement, gate_up_weight, down_weight):
    groups = N_GRP
    owners = N_EP
    experts = EXP_G
    capacity = CAP
    block_rows = TOK_DEV // groups
    order = jnp.argsort(destination, axis=-1).astype(jnp.int32)
    group_ids = jnp.arange(groups, dtype=jnp.int32)[:, None, None]
    owner_ids = jnp.arange(owners, dtype=jnp.int32)[None, :, None]
    slot_ids = jnp.arange(capacity, dtype=jnp.int32)[None, None, None, :]
    keep = (slot_ids < counts[:, :, :, None])[..., None]

    def rebalance(full):
        blocks = full.reshape(groups, owners, groups, block_rows, D)
        moved = blocks[group_ids, owner_ids, order]
        moved = jnp.transpose(moved, (2, 1, 0, 3, 4)).reshape(groups, owners, experts, capacity, D)
        return jnp.where(keep, moved, jnp.zeros((), moved.dtype))

    kept_tokens = rebalance(tokens)
    kept_cotangent = rebalance(cotangent)
    expert_of = (placement // SPLIT).astype(jnp.int32)
    owner_table = (expert_of[:, None] == jnp.arange(experts, dtype=jnp.int32)[None, :]).astype(jnp.float32)
    gate_up_full = gate_up_weight.astype(jnp.float32)
    down_full = down_weight.astype(jnp.float32)

    def per_group(carry, pair):
        here_tokens, here_cotangent = pair
        slot_tokens = jnp.transpose(jnp.take(here_tokens, expert_of, axis=1), (1, 0, 2, 3))
        slot_tokens = slot_tokens.reshape(owners, owners * capacity, D).astype(jnp.float32)
        slot_cotangent = jnp.transpose(jnp.take(here_cotangent, expert_of, axis=1), (1, 0, 2, 3))
        slot_cotangent = slot_cotangent.reshape(owners, owners * capacity, D).astype(jnp.float32)
        gate_up = jnp.einsum("jrd,jkds->jkrs", slot_tokens, gate_up_full)
        hidden_grad = jnp.einsum("jrd,jds->jrs", slot_cotangent, down_full)
        hidden, grad_rows = jax.vmap(swiglu_backward)(gate_up, hidden_grad)
        hidden_wide = hidden.astype(jnp.float32)
        grad_wide = grad_rows.astype(jnp.float32)
        forward_part = jnp.einsum("jrs,jds->jrd", hidden_wide, down_full).astype(jnp.bfloat16)
        backward_part = jnp.einsum("jkrs,jkds->jrd", grad_wide, gate_up_full).astype(jnp.bfloat16)
        forward_part = widen(forward_part).reshape(owners, owners, capacity, D)
        backward_part = widen(backward_part).reshape(owners, owners, capacity, D)
        layer_rows = jnp.einsum("jkcd,je->kecd", forward_part, owner_table).astype(jnp.bfloat16)
        grad_rows_out = jnp.einsum("jkcd,je->kecd", backward_part, owner_table).astype(jnp.bfloat16)
        gate_up_term = jnp.einsum("jrd,jkrs->jkds", slot_tokens, grad_wide).astype(jnp.bfloat16)
        down_term = jnp.einsum("jrd,jrs->jds", slot_cotangent, hidden_wide).astype(jnp.bfloat16)
        gate_up_sum = carry[0] + widen(gate_up_term)
        down_sum = carry[1] + widen(down_term)
        outputs = (layer_rows.reshape(owners, TOK_DEV, D), grad_rows_out.reshape(owners, TOK_DEV, D))
        return (gate_up_sum, down_sum), outputs

    initial = (jnp.zeros((owners, 2, D, SLICE), jnp.float32), jnp.zeros((owners, D, SLICE), jnp.float32))
    sums, stacked = lax.scan(per_group, initial, (kept_tokens, kept_cotangent))
    layer_out = stacked[0].reshape(groups, owners * TOK_DEV, D)
    input_grad = stacked[1].reshape(groups, owners * TOK_DEV, D)
    return (layer_out, input_grad, sums[0], sums[1])
```

```python
import functools

import jax
import jax.numpy as jnp
import numpy as np
from jax import lax
from jax.experimental import pallas as pl
from jax.experimental.pallas import tpu as pltpu
from jax.sharding import PartitionSpec as P

MESH = pl.DeviceIdType.MESH
BF16 = jnp.bfloat16
F32 = jnp.float32
PAIR = 2


def dot(a, b, contract):
    return lax.dot_general(a, b, ((contract[:1], contract[1:]), ((), ())), preferred_element_type=F32)


def kernel(
    dims,
    packed_ref, meta_ref, expert_ref, gate_up_ref, down_ref,
    rows_out, gate_up_out, down_out,
    inbox, metas, xall, weights, part, partin, grads, outrows, yin, zin, own, outbox, inbox2, gate_up_acc, down_acc,
    pack_sems, meta_sems, z_sems, y_sems, part_sems, grad_sems, yo_sems, zo_sems, out_sems, w_sems, o_sems,
):
    groups, zs, fold, tok, experts, split, per_dot = dims
    me, ep = lax.axis_index("grp"), lax.axis_index("ep")
    z, y = ep // PAIR, ep % PAIR
    other = z * PAIR + (PAIR - 1 - y)
    width, cols, slc = xall.shape[-1], inbox.shape[-1], down_acc.shape[-1]
    rows = xall.shape[3]
    blocks = PAIR * zs
    per_chunk = blocks // groups
    n_in, n_rows = groups * inbox.shape[1], 2 * rows

    loads = [
        pltpu.make_async_copy(gate_up_ref.at[0], weights.at[:, pl.ds(0, slc)], w_sems.at[0]),
        pltpu.make_async_copy(gate_up_ref.at[1], weights.at[:, pl.ds(slc, slc)], w_sems.at[1]),
        pltpu.make_async_copy(down_ref, weights.at[:, pl.ds(2 * slc, slc)], w_sems.at[2]),
    ]
    for load in loads:
        load.start()

    grp_peers = [(d, lax.rem(me + d, groups)) for d in range(1, groups)]
    z_peers = [(d, lax.rem(z + d, zs)) for d in range(1, zs)]

    barrier = pltpu.get_barrier_semaphore()
    for _, p in grp_peers:
        pl.semaphore_signal(barrier, inc=1, device_id=(p, ep), device_id_type=MESH)
    for _, q in z_peers:
        pl.semaphore_signal(barrier, inc=1, device_id=(me, q * PAIR + y), device_id_type=MESH)
    pl.semaphore_signal(barrier, inc=1, device_id=(me, other), device_id_type=MESH)
    pl.semaphore_wait(barrier, groups - 1 + zs - 1 + 1)

    def remote(src, dst, sems, at, device):
        return pltpu.make_async_remote_copy(
            src_ref=src, dst_ref=dst, send_sem=sems.at[0, at], recv_sem=sems.at[1, at],
            device_id=device, device_id_type=MESH,
        )

    sent = []

    meta_copies = [remote(meta_ref, metas.at[me], meta_sems, d, (p, ep)) for d, p in grp_peers]
    pack_copies = [remote(packed_ref.at[p], inbox.at[me], pack_sems, d, (p, ep)) for d, p in grp_peers]
    for copy in meta_copies + pack_copies:
        copy.start()
    sent += meta_copies + pack_copies
    metas[me] = meta_ref[...]
    inbox[me] = packed_ref[me]
    for copy in meta_copies:
        copy.wait_recv()

    def meta_row(g, at, count):
        return metas[g, at:at + 1, 0:count]

    dest_in = sum(meta_row(g, 0, n_in) for g in range(groups))
    dest_rows = sum(meta_row(g, 2, n_rows) for g in range(groups))
    row_of, fold_of, slot_of = (meta_ref[i:i + 1, 0:n_in] for i in (3, 4, 5))
    base = meta_ref[6:7, 0:n_rows]
    kept = sum(
        jnp.where((dest_in == h) & (slot_of < meta_row(h, 1, n_in)), 1, 0) for h in range(groups)
    )
    row_of = jnp.where(kept > 0, row_of, -1)
    row_at = lax.broadcasted_iota(jnp.int32, (n_rows, n_in), 0)
    picks_in = [
        jnp.where((row_at == row_of) & (fold_of == f), 1.0, 0.0).astype(BF16) for f in range(fold)
    ]
    out_at = lax.broadcasted_iota(jnp.int32, (n_in, n_rows), 0)
    target = dest_rows * (fold * 2 * tok) + base
    picks_out = [
        jnp.where(out_at == target + f * 2 * tok, 1.0, 0.0).astype(BF16) for f in range(fold)
    ]

    for copy in pack_copies:
        copy.wait_recv()
    arrived = inbox[...].reshape(n_in, cols)
    for f in range(fold):
        picked = dot(picks_in[f], arrived, (1, 0)).astype(BF16)
        xall[0, z, :, :, f * cols:(f + 1) * cols] = picked.reshape(2, rows, cols)

    y_own = remote(xall.at[0, z], xall.at[1, z], y_sems, 0, (me, other))
    y_own.start()
    z_copies = [
        remote(xall.at[0, z], xall.at[0, z], z_sems, d, (me, q * PAIR + y)) for d, q in z_peers
    ]
    for copy in z_copies:
        copy.start()
    y_copies = [y_own]
    for d, copy in zip(range(1, zs), z_copies):
        copy.wait_recv()
        source = lax.rem(z + zs - d, zs)
        forward = remote(xall.at[0, source], xall.at[1, source], y_sems, d, (me, other))
        forward.start()
        y_copies.append(forward)
    sent += z_copies + y_copies

    for load in loads:
        load.wait()

    def x_rows(side, first, kind):
        return xall[side, pl.ds(first, per_dot), kind].reshape(per_dot * rows, width)

    def project(side):
        def step(i, carry):
            first = i * per_dot
            gate_up = dot(x_rows(side, first, 0), weights[:, 0:2 * slc], (1, 0))
            hidden_grad = dot(x_rows(side, first, 1), weights[:, 2 * slc:3 * slc], (1, 0))
            at = pl.ds(side * zs + first, per_dot)
            part[at, :, 0:2 * slc] = gate_up.astype(BF16).reshape(per_dot, rows, 2 * slc)
            part[at, :, 2 * slc:3 * slc] = hidden_grad.astype(BF16).reshape(per_dot, rows, slc)
            return carry

        lax.fori_loop(0, zs // per_dot, step, 0)

    project(0)
    for copy in y_copies:
        copy.wait_recv()
    project(1)

    part_copies = [
        remote(part.at[pl.ds(p * per_chunk, per_chunk)], partin.at[me], part_sems, d, (p, ep))
        for d, p in grp_peers
    ]
    for copy in part_copies:
        copy.start()
    sent += part_copies
    total = part[pl.ds(me * per_chunk, per_chunk)].astype(F32)
    for d, copy in zip(range(1, groups), part_copies):
        copy.wait_recv()
        total = total + partin[lax.rem(me + groups - d, groups)].astype(F32)
    gate, up, hidden_grad = (total[:, :, i * slc:(i + 1) * slc] for i in range(3))
    sig = jax.nn.sigmoid(gate)
    activated = gate * sig
    hidden = activated * up
    gate_grad = hidden_grad * up * sig * (1.0 + gate * (1.0 - sig))
    up_grad = hidden_grad * activated
    if experts > 1:
        row = lax.broadcasted_iota(jnp.int32, gate.shape, 1)
        block = tok // groups
        slot = (row // tok) * block + row % block
        mine = slot // (tok // experts) == expert_ref[0]
        gate_grad, up_grad, hidden = (jnp.where(mine, v, 0.0) for v in (gate_grad, up_grad, hidden))
    share = pl.ds(me * per_chunk, per_chunk)
    grads[share, :, 0:slc] = gate_grad.astype(BF16)
    grads[share, :, slc:2 * slc] = up_grad.astype(BF16)
    grads[share, :, 2 * slc:3 * slc] = hidden.astype(BF16)
    grad_copies = [
        remote(grads.at[share], grads.at[share], grad_sems, d, (p, ep)) for d, p in grp_peers
    ]
    for copy in grad_copies:
        copy.start()
    sent += grad_copies
    for copy in grad_copies:
        copy.wait_recv()

    def grad_rows(side, first, low, high):
        count = (high - low) * slc
        return grads[pl.ds(side * zs + first, per_dot), :, low * slc:high * slc].reshape(per_dot * rows, count)

    def to_other(i, carry):
        first = i * per_dot
        at = pl.ds(first, per_dot)
        ahead = dot(grad_rows(1, first, 2, 3), weights[:, 2 * slc:3 * slc], (1, 1))
        back = dot(grad_rows(1, first, 0, 2), weights[:, 0:2 * slc], (1, 1))
        outrows[at, 0] = ahead.astype(BF16).reshape(per_dot, rows, width)
        outrows[at, 1] = back.astype(BF16).reshape(per_dot, rows, width)
        return carry

    lax.fori_loop(0, zs // per_dot, to_other, 0)
    order = [lax.rem(z + d, zs) for d in list(range(1, zs)) + [0]]
    yo_copies = [
        remote(outrows.at[q], yin.at[q], yo_sems, i, (me, other)) for i, q in enumerate(order)
    ]
    for copy in yo_copies:
        copy.start()

    gate_up_acc[...] = jnp.zeros_like(gate_up_acc)
    down_acc[...] = jnp.zeros_like(down_acc)
    for side in range(PAIR):
        def weight_step(i, carry, side=side):
            first = i * per_dot
            both = dot(x_rows(side, first, 0), grad_rows(side, first, 0, 2), (0, 0))
            gate_up_acc[0] += both[:, 0:slc]
            gate_up_acc[1] += both[:, slc:2 * slc]
            down_acc[...] += dot(x_rows(side, first, 1), grad_rows(side, first, 2, 3), (0, 0))
            return carry

        lax.fori_loop(0, zs // per_dot, weight_step, 0)
    stores = [
        pltpu.make_async_copy(gate_up_acc, gate_up_out, o_sems.at[0]),
        pltpu.make_async_copy(down_acc, down_out, o_sems.at[1]),
    ]
    for store in stores:
        store.start()

    zo_copies = []
    for i, q in enumerate(order):
        at = pl.ds(q, 1)
        h = grads[at, :, 2 * slc:3 * slc].reshape(rows, slc)
        gu = grads[at, :, 0:2 * slc].reshape(rows, 2 * slc)
        ahead = dot(h, weights[:, 2 * slc:3 * slc], (1, 1))
        back = dot(gu, weights[:, 0:2 * slc], (1, 1))
        yo_copies[i].wait()
        ahead = ahead + yin[q, 0].astype(F32)
        back = back + yin[q, 1].astype(F32)
        if i < zs - 1:
            outrows[q, 0] = ahead.astype(BF16)
            outrows[q, 1] = back.astype(BF16)
            copy = remote(outrows.at[q], zin.at[z], zo_sems, i + 1, (me, q * PAIR + y))
            copy.start()
            zo_copies.append(copy)
        else:
            own[0] = ahead
            own[1] = back
    sent += zo_copies
    for d, copy in zip(range(1, zs), zo_copies):
        copy.wait_recv()
        own[...] += zin[lax.rem(z + zs - d, zs)].astype(F32)

    final = own[...].astype(BF16).reshape(n_rows, width)
    placed = sum(
        dot(picks_out[f], final[:, f * cols:(f + 1) * cols], (1, 0)) for f in range(fold)
    )
    outbox[...] = placed.astype(BF16).reshape(outbox.shape)
    out_copies = [remote(outbox.at[p], inbox2.at[me], out_sems, d, (p, ep)) for d, p in grp_peers]
    for copy in out_copies:
        copy.start()
    sent += out_copies
    inbox2[me] = outbox[me]
    for copy in out_copies:
        copy.wait_recv()
    rows_out[...] = inbox2[...]
    for store in stores:
        store.wait()
    for copy in sent:
        copy.wait_send()


def body(tokens, cotangent, counts, destination, placement, gate_up_weight, down_weight):
    groups = lax.axis_size("grp")
    owners = lax.axis_size("ep")
    me, ep = lax.axis_index("grp"), lax.axis_index("ep")
    tok, model = tokens.shape[1], tokens.shape[2]
    experts = counts.shape[2]
    cap = tok // experts
    block = tok // groups
    split = owners // experts
    width, slc = down_weight.shape[1], down_weight.shape[2]
    zs = owners // PAIR
    fold = max(1, 16 // (2 * tok))
    cols = width // fold
    box = fold * 2 * tok
    rows = groups * tok
    n_in, n_rows = groups * box, 2 * rows
    per_dot = min(zs, max(1, 64 // rows))
    lanes = -(-max(n_in, n_rows) // 128) * 128

    def pad(values, fill):
        return np.concatenate([values, np.full(lanes - len(values), fill)]).astype(np.int32)

    g_i, f_i, t_i, q_i = (v.ravel() for v in np.indices((groups, fold, 2, tok)))
    t_m, g_m, q_m = (v.ravel() for v in np.indices((2, groups, tok)))
    slot_i = g_i * block + q_i % block
    slot_m = g_m * block + q_m % block
    dest = destination[0, 0]
    kept_count = counts[0, 0]
    zero = np.zeros(lanes, np.int32)
    meta = jnp.stack([
        jnp.where(pad(g_i, -1) == me, dest[pad(q_i // block, 0)], 0),
        kept_count[pad(slot_i // cap, 0)],
        jnp.where(pad(g_m, -1) == me, dest[pad(q_m // block, 0)], 0),
        pad(t_i * rows + g_i * tok + q_i, -1),
        pad(f_i, -1),
        pad(slot_i % cap, 0),
        pad(t_m * tok + slot_m, 0),
        zero,
    ])
    packed = jnp.stack([tokens[0], cotangent[0]]).reshape(2, tok, groups, fold, cols)
    packed = jnp.transpose(packed, (2, 3, 0, 1, 4)).reshape(groups, box, cols)
    expert = lax.dynamic_slice(placement // split, (ep,), (1,))

    blocks = PAIR * zs
    per_chunk = blocks // groups
    vmem = pl.BlockSpec(memory_space=pltpu.VMEM)
    anywhere = pl.BlockSpec(memory_space=pl.ANY)
    shapes = [
        ((groups, box, cols), BF16),
        ((groups, 8, lanes), jnp.int32),
        ((PAIR, zs, 2, rows, width), BF16),
        ((width, 3 * slc), BF16),
        ((blocks, rows, 3 * slc), BF16),
        ((groups, per_chunk, rows, 3 * slc), BF16),
        ((blocks, rows, 3 * slc), BF16),
        ((zs, 2, rows, width), BF16),
        ((zs, 2, rows, width), BF16),
        ((zs, 2, rows, width), BF16),
        ((2, rows, width), F32),
        ((groups, box, cols), BF16),
        ((groups, box, cols), BF16),
        ((2, width, slc), F32),
        ((width, slc), F32),
    ]
    held = sum(
        int(np.prod(s[:-1])) * (-(-s[-1] // 128) * 128) * np.dtype(t).itemsize for s, t in shapes
    )
    dma = pltpu.SemaphoreType.DMA
    out, gate_up_grad, down_grad = pl.pallas_call(
        functools.partial(kernel, (groups, zs, fold, tok, experts, split, per_dot)),
        out_shape=(
            jax.ShapeDtypeStruct((groups, box, cols), BF16),
            jax.ShapeDtypeStruct((2, width, slc), F32),
            jax.ShapeDtypeStruct((width, slc), F32),
        ),
        in_specs=[vmem, vmem, pl.BlockSpec(memory_space=pltpu.SMEM), anywhere, anywhere],
        out_specs=(vmem, anywhere, anywhere),
        scratch_shapes=[pltpu.VMEM(s, t) for s, t in shapes] + [
            dma((2, groups)), dma((2, groups)), dma((2, zs)), dma((2, zs)), dma((2, groups)),
            dma((2, groups)), dma((2, zs)), dma((2, zs)), dma((2, groups)), dma((3,)), dma((2,)),
        ],
        compiler_params=pltpu.CompilerParams(
            collective_id=0, has_side_effects=True, vmem_limit_bytes=min(held + (12 << 20), 62 << 20)
        ),
    )(packed, meta, expert, gate_up_weight[0], down_weight[0])
    out = out.reshape(groups, fold, 2, tok, cols)
    out = jnp.transpose(out, (2, 3, 0, 1, 4)).reshape(2, 1, tok, model)
    return out[0], out[1], gate_up_grad[None], down_grad[None]


def solution(mesh):
    return jax.shard_map(
        body,
        mesh=mesh,
        in_specs=(
            P("grp", "ep", None),
            P("grp", "ep", None),
            P("grp", "ep", None),
            P("grp", "ep", None),
            P(),
            P("ep", None, "grp", None),
            P("ep", "grp", None),
        ),
        out_specs=(
            P("grp", "ep", None),
            P("grp", "ep", None),
            P("ep", None, "grp", None),
            P("ep", "grp", None),
        ),
        check_vma=False,
    )
```

```python
import functools

import jax
import jax.numpy as jnp
import numpy as np
from jax import lax
from jax.experimental import pallas as pl
from jax.experimental.pallas import tpu as pltpu
from jax.sharding import PartitionSpec as P

MESH = pl.DeviceIdType.MESH
BF16 = jnp.bfloat16
F32 = jnp.float32
PAIR = 2


def dot(a, b, contract):
    return lax.dot_general(a, b, ((contract[:1], contract[1:]), ((), ())), preferred_element_type=F32)


def kernel(
    dims,
    packed_ref, dest_ref, counts_ref, placement_ref, gate_up_ref, down_ref,
    rows_out, gate_up_out, down_out,
    inbox, metas, xall, weights, part, partin, grads, outrows, mine, yin, zin, own, outbox, inbox2, gate_up_acc, down_acc,
    pack_sems, meta_sems, z_sems, y_sems, part_sems, grad_sems, yo_sems, zo_sems, out_sems, w_sems, o_sems,
):
    groups, zs, fold, tok, experts, split, per_dot = dims
    me, ep = lax.axis_index("grp"), lax.axis_index("ep")
    z, y = ep // PAIR, ep % PAIR
    other = z * PAIR + (PAIR - 1 - y)
    width, cols, slc = xall.shape[-1], inbox.shape[-1], down_acc.shape[-1]
    rows = xall.shape[3]
    block, cap = tok // groups, tok // experts
    share = zs // groups
    box = inbox.shape[1]
    n_in, n_rows = groups * box, 2 * rows

    grp_peers = [(d, lax.rem(me + d, groups)) for d in range(1, groups)]
    z_peers = [(d, lax.rem(z + d, zs)) for d in range(1, zs)]

    barrier = pltpu.get_barrier_semaphore()
    for _, p in grp_peers:
        pl.semaphore_signal(barrier, inc=1, device_id=(p, ep), device_id_type=MESH)
    for _, q in z_peers:
        pl.semaphore_signal(barrier, inc=1, device_id=(me, q * PAIR + y), device_id_type=MESH)
    pl.semaphore_signal(barrier, inc=1, device_id=(me, other), device_id_type=MESH)

    loads = [
        pltpu.make_async_copy(gate_up_ref.at[0], weights.at[:, pl.ds(0, slc)], w_sems.at[0]),
        pltpu.make_async_copy(gate_up_ref.at[1], weights.at[:, pl.ds(slc, slc)], w_sems.at[1]),
        pltpu.make_async_copy(down_ref, weights.at[:, pl.ds(2 * slc, slc)], w_sems.at[2]),
    ]
    for load in loads:
        load.start()

    lanes = metas.shape[-1]
    lane = lax.broadcasted_iota(jnp.int32, (8, lanes), 1)
    line = lax.broadcasted_iota(jnp.int32, (8, lanes), 0)

    def slots(group, row):
        return group * block + lax.rem(row, block)

    lane_block = lax.div(lax.rem(lane, tok), block)
    lane_expert = lax.div(slots(lax.div(lane, box), lax.rem(lane, tok)), cap)
    own_dest = sum(jnp.where(lane_block == b, dest_ref[0, 0, b], 0) for b in range(groups))
    own_count = sum(jnp.where(lane_expert == e, counts_ref[0, 0, e], 0) for e in range(experts))
    metas[me] = jnp.where(line == 0, own_dest, own_count)
    inbox[me] = packed_ref[me]

    pl.semaphore_wait(barrier, groups - 1 + zs - 1 + 1)

    def remote(src, dst, sems, at, device):
        return pltpu.make_async_remote_copy(
            src_ref=src, dst_ref=dst, send_sem=sems.at[0, at], recv_sem=sems.at[1, at],
            device_id=device, device_id_type=MESH,
        )

    sent = []

    meta_copies = [remote(metas.at[me], metas.at[me], meta_sems, d, (p, ep)) for d, p in grp_peers]
    pack_copies = [remote(packed_ref.at[p], inbox.at[me], pack_sems, d, (p, ep)) for d, p in grp_peers]
    for copy in meta_copies + pack_copies:
        copy.start()
    sent += meta_copies + pack_copies

    n = lax.broadcasted_iota(jnp.int32, (1, n_in), 1)
    n_group, n_row = lax.div(n, box), lax.rem(n, tok)
    n_fold = lax.div(lax.rem(n, box), 2 * tok)
    row_of = lax.rem(lax.div(n, tok), 2) * rows + n_group * tok + n_row
    slot_of = lax.rem(slots(n_group, n_row), cap)
    m = lax.broadcasted_iota(jnp.int32, (1, n_rows), 1)
    m_group = lax.rem(lax.div(m, tok), groups)
    base = lax.div(m, rows) * tok + slots(m_group, lax.rem(m, tok))
    row_at = lax.broadcasted_iota(jnp.int32, (n_rows, n_in), 0)
    out_at = lax.broadcasted_iota(jnp.int32, (n_in, n_rows), 0)

    for copy in meta_copies:
        copy.wait_recv()
    dest_in = sum(jnp.where(n_group == g, metas[g, 0:1, 0:n_in], 0) for g in range(groups))
    dest_rows = sum(jnp.where(m_group == g, metas[g, 0:1, 0:n_rows], 0) for g in range(groups))
    kept = sum(
        jnp.where((dest_in == h) & (slot_of < metas[h, 1:2, 0:n_in]), 1, 0) for h in range(groups)
    )
    row_of = jnp.where(kept > 0, row_of, -1)
    picks_in = [
        jnp.where((row_at == row_of) & (n_fold == f), 1.0, 0.0).astype(BF16) for f in range(fold)
    ]

    for copy in pack_copies:
        copy.wait_recv()
    arrived = inbox[...].reshape(n_in, cols)
    for f in range(fold):
        picked = dot(picks_in[f], arrived, (1, 0)).astype(BF16)
        xall[0, z, :, :, f * cols:(f + 1) * cols] = picked.reshape(2, rows, cols)

    z_copies, y_copies = [[], []], [[], []]
    for t in range(2):
        y_copies[t].append(remote(xall.at[0, z, t], xall.at[1, z, t], y_sems, t * zs, (me, other)))
        z_copies[t] = [
            remote(xall.at[0, z, t], xall.at[0, z, t], z_sems, t * zs + d, (me, q * PAIR + y))
            for d, q in z_peers
        ]
        for copy in y_copies[t] + z_copies[t]:
            copy.start()

    def pass_on(t):
        for d, copy in zip(range(1, zs), z_copies[t]):
            copy.wait_recv()
            source = lax.rem(z + zs - d, zs)
            forward = remote(
                xall.at[0, source, t], xall.at[1, source, t], y_sems, t * zs + d, (me, other)
            )
            forward.start()
            y_copies[t].append(forward)

    def x_rows(side, first, kind):
        return xall[side, pl.ds(first, per_dot), kind].reshape(per_dot * rows, width)

    def project(side, kind):
        low, high = ((0, 2), (2, 3))[kind]

        def step(i, carry):
            first = i * per_dot
            out = dot(x_rows(side, first, kind), weights[:, low * slc:high * slc], (1, 0))
            part[side, pl.ds(first, per_dot), :, low * slc:high * slc] = (
                out.astype(BF16).reshape(per_dot, rows, (high - low) * slc)
            )
            return carry

        lax.fori_loop(0, zs // per_dot, step, 0)

    def send_parts(side):
        copies = [
            remote(
                part.at[side, pl.ds(p * share, share)], partin.at[side, me],
                part_sems, side * groups + d, (p, ep),
            )
            for d, p in grp_peers
        ]
        for copy in copies:
            copy.start()
        return copies

    held = pl.ds(me * share, share)

    def activate(side, copies):
        total = part[side, held].astype(F32)
        for d, copy in zip(range(1, groups), copies):
            copy.wait_recv()
            total = total + partin[side, lax.rem(me + groups - d, groups)].astype(F32)
        gate, up, hidden_grad = (total[:, :, i * slc:(i + 1) * slc] for i in range(3))
        sig = jax.nn.sigmoid(gate)
        activated = gate * sig
        hidden = activated * up
        gate_grad = hidden_grad * up * sig * (1.0 + gate * (1.0 - sig))
        up_grad = hidden_grad * activated
        if experts > 1:
            row = lax.broadcasted_iota(jnp.int32, gate.shape, 1)
            slot = slots(lax.div(row, tok), lax.rem(row, tok))
            served = lax.div(slot, cap) == lax.div(placement_ref[ep], split)
            gate_grad, up_grad, hidden = (
                jnp.where(served, v, 0.0) for v in (gate_grad, up_grad, hidden)
            )
        grads[side, held, :, 0:slc] = gate_grad.astype(BF16)
        grads[side, held, :, slc:2 * slc] = up_grad.astype(BF16)
        grads[side, held, :, 2 * slc:3 * slc] = hidden.astype(BF16)
        result = [
            remote(
                grads.at[side, held], grads.at[side, held],
                grad_sems, side * groups + d, (p, ep),
            )
            for d, p in grp_peers
        ]
        for copy in result:
            copy.start()
        return result

    def grad_rows(side, first, low, high):
        count = (high - low) * slc
        return grads[side, pl.ds(first, per_dot), :, low * slc:high * slc].reshape(per_dot * rows, count)

    def produce(side, target):
        def step(i, carry):
            first = i * per_dot
            at = pl.ds(first, per_dot)
            ahead = dot(grad_rows(side, first, 2, 3), weights[:, 2 * slc:3 * slc], (1, 1))
            target[at, 0] = ahead.astype(target.dtype).reshape(per_dot, rows, width)
            back = dot(grad_rows(side, first, 0, 2), weights[:, 0:2 * slc], (1, 1))
            target[at, 1] = back.astype(target.dtype).reshape(per_dot, rows, width)
            return carry

        lax.fori_loop(0, zs // per_dot, step, 0)

    def weight_grads(side):
        def step(i, carry):
            first = i * per_dot
            both = dot(x_rows(side, first, 0), grad_rows(side, first, 0, 2), (0, 0))
            down = dot(x_rows(side, first, 1), grad_rows(side, first, 2, 3), (0, 0))
            if side == 0 and zs == per_dot:
                gate_up_acc[0] = both[:, 0:slc]
                gate_up_acc[1] = both[:, slc:2 * slc]
                down_acc[...] = down
            else:
                gate_up_acc[0] += both[:, 0:slc]
                gate_up_acc[1] += both[:, slc:2 * slc]
                down_acc[...] += down
            return carry

        if side == 0 and zs != per_dot:
            gate_up_acc[...] = jnp.zeros_like(gate_up_acc)
            down_acc[...] = jnp.zeros_like(down_acc)
        lax.fori_loop(0, zs // per_dot, step, 0)

    pass_on(0)
    for load in loads:
        load.wait()
    project(0, 0)
    pass_on(1)
    project(0, 1)
    first_parts = send_parts(0)
    first_grads = activate(0, first_parts)
    for t in range(2):
        for copy in y_copies[t]:
            copy.wait_recv()
        project(1, t)
    second_parts = send_parts(1)
    for copy in first_grads:
        copy.wait_recv()
    produce(0, mine)
    second_grads = activate(1, second_parts)
    weight_grads(0)
    for copy in second_grads:
        copy.wait_recv()
    for t in range(2):
        sent += z_copies[t] + y_copies[t]
    sent += first_parts + second_parts + first_grads + second_grads

    produce(1, outrows)
    order = [lax.rem(z + d, zs) for d in list(range(1, zs)) + [0]]
    yo_copies = [
        remote(outrows.at[q], yin.at[q], yo_sems, i, (me, other)) for i, q in enumerate(order)
    ]
    for copy in yo_copies:
        copy.start()
    zo_copies = []
    for i, q in enumerate(order):
        yo_copies[i].wait()
        if i < zs - 1:
            outrows[q] = (mine[q].astype(F32) + yin[q].astype(F32)).astype(BF16)
            copy = remote(outrows.at[q], zin.at[z], zo_sems, i + 1, (me, q * PAIR + y))
            copy.start()
            zo_copies.append(copy)
        else:
            own[...] = mine[q].astype(F32) + yin[q].astype(F32)
    sent += zo_copies

    weight_grads(1)
    stores = [
        pltpu.make_async_copy(gate_up_acc, gate_up_out, o_sems.at[0]),
        pltpu.make_async_copy(down_acc, down_out, o_sems.at[1]),
    ]
    for store in stores:
        store.start()
    target = dest_rows * (fold * 2 * tok) + base
    picks_out = [
        jnp.where(out_at == target + f * 2 * tok, 1.0, 0.0).astype(BF16) for f in range(fold)
    ]

    for d, copy in zip(range(1, zs), zo_copies):
        copy.wait_recv()
        own[...] += zin[lax.rem(z + zs - d, zs)].astype(F32)

    final = own[...].astype(BF16).reshape(n_rows, width)
    placed = sum(
        dot(picks_out[f], final[:, f * cols:(f + 1) * cols], (1, 0)) for f in range(fold)
    )
    outbox[...] = placed.astype(BF16).reshape(outbox.shape)
    out_copies = [remote(outbox.at[p], inbox2.at[me], out_sems, d, (p, ep)) for d, p in grp_peers]
    for copy in out_copies:
        copy.start()
    sent += out_copies
    inbox2[me] = outbox[me]
    for copy in out_copies:
        copy.wait_recv()
    rows_out[...] = inbox2[...]
    for store in stores:
        store.wait()
    for copy in sent:
        copy.wait_send()


def body(tokens, cotangent, counts, destination, placement, gate_up_weight, down_weight):
    groups = lax.axis_size("grp")
    owners = lax.axis_size("ep")
    tok, model = tokens.shape[1], tokens.shape[2]
    experts = counts.shape[2]
    split = owners // experts
    width, slc = down_weight.shape[1], down_weight.shape[2]
    zs = owners // PAIR
    fold = max(1, 16 // (2 * tok))
    cols = width // fold
    box = fold * 2 * tok
    rows = groups * tok
    n_in, n_rows = groups * box, 2 * rows
    per_dot = min(zs, max(1, 64 // rows))
    lanes = -(-max(n_in, n_rows) // 128) * 128

    packed = jnp.stack([tokens[0], cotangent[0]]).reshape(2, tok, groups, fold, cols)
    packed = jnp.transpose(packed, (2, 3, 0, 1, 4)).reshape(groups, box, cols)

    share = zs // groups
    vmem = pl.BlockSpec(memory_space=pltpu.VMEM)
    smem = pl.BlockSpec(memory_space=pltpu.SMEM)
    anywhere = pl.BlockSpec(memory_space=pl.ANY)
    shapes = [
        ((groups, box, cols), BF16),
        ((groups, 8, lanes), jnp.int32),
        ((PAIR, zs, 2, rows, width), BF16),
        ((width, 3 * slc), BF16),
        ((PAIR, zs, rows, 3 * slc), BF16),
        ((PAIR, groups, share, rows, 3 * slc), BF16),
        ((PAIR, zs, rows, 3 * slc), BF16),
        ((zs, 2, rows, width), BF16),
        ((zs, 2, rows, width), F32 if zs * rows * width < (1 << 20) else BF16),
        ((zs, 2, rows, width), BF16),
        ((zs, 2, rows, width), BF16),
        ((2, rows, width), F32),
        ((groups, box, cols), BF16),
        ((groups, box, cols), BF16),
        ((2, width, slc), F32),
        ((width, slc), F32),
    ]
    dma = pltpu.SemaphoreType.DMA
    out, gate_up_grad, down_grad = pl.pallas_call(
        functools.partial(kernel, (groups, zs, fold, tok, experts, split, per_dot)),
        out_shape=(
            jax.ShapeDtypeStruct((groups, box, cols), BF16),
            jax.ShapeDtypeStruct((2, width, slc), F32),
            jax.ShapeDtypeStruct((width, slc), F32),
        ),
        in_specs=[vmem, smem, smem, smem, anywhere, anywhere],
        out_specs=(vmem, anywhere, anywhere),
        scratch_shapes=[pltpu.VMEM(s, t) for s, t in shapes] + [
            dma((2, groups)), dma((2, groups)), dma((2, 2 * zs)), dma((2, 2 * zs)), dma((2, PAIR * groups)),
            dma((2, PAIR * groups)), dma((2, zs)), dma((2, zs)), dma((2, groups)), dma((3,)), dma((2,)),
        ],
        compiler_params=pltpu.CompilerParams(
            collective_id=0, has_side_effects=True, vmem_limit_bytes=60 << 20
        ),
    )(packed, destination, counts, placement, gate_up_weight[0], down_weight[0])
    out = out.reshape(groups, fold, 2, tok, cols)
    out = jnp.transpose(out, (2, 3, 0, 1, 4)).reshape(2, 1, tok, model)
    return out[0], out[1], gate_up_grad[None], down_grad[None]


def solution(mesh):
    return jax.shard_map(
        body,
        mesh=mesh,
        in_specs=(
            P("grp", "ep", None),
            P("grp", "ep", None),
            P("grp", "ep", None),
            P("grp", "ep", None),
            P(),
            P("ep", None, "grp", None),
            P("ep", "grp", None),
        ),
        out_specs=(
            P("grp", "ep", None),
            P("grp", "ep", None),
            P("ep", None, "grp", None),
            P("ep", "grp", None),
        ),
        check_vma=False,
    )
```

```python
import functools

import jax
import jax.numpy as jnp
import numpy as np
from jax import lax
from jax.experimental import pallas as pl
from jax.experimental.pallas import tpu as pltpu
from jax.sharding import PartitionSpec as P

MESH = pl.DeviceIdType.MESH
BF16 = jnp.bfloat16
F32 = jnp.float32
PAIR = 2


def dot(a, b, contract):
    return lax.dot_general(a, b, ((contract[:1], contract[1:]), ((), ())), preferred_element_type=F32)


def kernel(
    dims,
    tokens_ref, cotangent_ref, dest_ref, counts_ref, placement_ref, gate_up_ref, down_ref,
    rows_out, grads_out,
    inbox, metas, xall, weights, part_gu, part_h, in_gu, in_h, hidden, grads, outrows, mine, yin, zin, own, outbox, inbox2, acc,
    pack_sems, meta_sems, up_sems, down_sems, y_sems, part_sems, grad_sems, yo_sems, zo_sems, out_sems, w_sems, o_sems,
):
    groups, zs, fold, tok, experts, split, per_dot = dims
    me, ep = lax.axis_index("grp"), lax.axis_index("ep")
    z, y = ep // PAIR, ep % PAIR
    other = z * PAIR + (PAIR - 1 - y)
    width, slc = xall.shape[-1], hidden.shape[-1]
    cols, box = outbox.shape[-1], outbox.shape[1]
    rows = xall.shape[3]
    block, cap = tok // groups, tok // experts
    blocks = PAIR * zs
    share = blocks // groups
    n_in, n_rows = groups * 2 * tok, 2 * rows

    grp_peers = [(d, lax.rem(me + d, groups)) for d in range(1, groups)]
    z_peers = [(d, lax.rem(z + d, zs)) for d in range(1, zs)]

    barrier = pltpu.get_barrier_semaphore()
    for _, p in grp_peers:
        pl.semaphore_signal(barrier, inc=1, device_id=(p, ep), device_id_type=MESH)
    for _, q in z_peers:
        pl.semaphore_signal(barrier, inc=1, device_id=(me, q * PAIR + y), device_id_type=MESH)
    pl.semaphore_signal(barrier, inc=1, device_id=(me, other), device_id_type=MESH)

    def piece(ref, p):
        if ref.shape[0] == 1:
            return ref.at[0, :, pl.ds(pl.multiple_of(p * width, width), width)]
        return ref.at[p]

    loads = [
        pltpu.make_async_copy(piece(tokens_ref, me), inbox.at[me, 0], w_sems.at[3]),
        pltpu.make_async_copy(piece(cotangent_ref, me), inbox.at[me, 1], w_sems.at[4]),
        pltpu.make_async_copy(gate_up_ref.at[0], weights.at[:, pl.ds(0, slc)], w_sems.at[0]),
        pltpu.make_async_copy(gate_up_ref.at[1], weights.at[:, pl.ds(slc, slc)], w_sems.at[1]),
        pltpu.make_async_copy(down_ref, weights.at[:, pl.ds(2 * slc, slc)], w_sems.at[2]),
    ]
    for load in loads:
        load.start()

    lanes = metas.shape[-1]
    lane = lax.broadcasted_iota(jnp.int32, (8, lanes), 1)
    line = lax.broadcasted_iota(jnp.int32, (8, lanes), 0)

    def slots(group, row):
        return group * block + lax.rem(row, block)

    lane_row, lane_group = lax.rem(lane, tok), lax.rem(lax.div(lane, tok), groups)
    lane_block = lax.div(lane_row, block)
    lane_expert = lax.div(slots(lane_group, lane_row), cap)
    own_dest = sum(jnp.where(lane_block == b, dest_ref[0, 0, b], 0) for b in range(groups))
    own_count = sum(jnp.where(lane_expert == e, counts_ref[0, 0, e], 0) for e in range(experts))
    metas[me] = jnp.where(line == 0, own_dest, own_count)

    pl.semaphore_wait(barrier, groups - 1 + zs - 1 + 1)

    def remote(src, dst, sems, at, device):
        return pltpu.make_async_remote_copy(
            src_ref=src, dst_ref=dst, send_sem=sems.at[0, at], recv_sem=sems.at[1, at],
            device_id=device, device_id_type=MESH,
        )

    sent = []

    meta_copies = [remote(metas.at[me], metas.at[me], meta_sems, d, (p, ep)) for d, p in grp_peers]
    pack_copies = [
        [
            remote(piece(ref, p), inbox.at[me, t], pack_sems, t * groups + d, (p, ep))
            for d, p in grp_peers
        ]
        for t, ref in enumerate((tokens_ref, cotangent_ref))
    ]
    for copy in meta_copies + pack_copies[0] + pack_copies[1]:
        copy.start()
    sent += meta_copies + pack_copies[0] + pack_copies[1]

    m = lax.broadcasted_iota(jnp.int32, (1, n_rows), 1)
    m_kind, m_group, m_row = lax.div(m, rows), lax.rem(lax.div(m, tok), groups), lax.rem(m, tok)
    slot = slots(m_group, m_row)
    base = m_kind * tok + slot
    out_at = lax.broadcasted_iota(jnp.int32, (groups * box, n_rows), 0)
    row_at = lax.broadcasted_iota(jnp.int32, (rows, tok), 0)
    col_at = lax.broadcasted_iota(jnp.int32, (rows, tok), 1)

    for copy in meta_copies:
        copy.wait_recv()
    dest = sum(jnp.where(m_group == g, metas[g, 0:1, 0:n_rows], 0) for g in range(groups))
    kept = sum(
        jnp.where((dest == h) & (lax.rem(slot, cap) < metas[h, 1:2, 0:n_rows]), 1, 0)
        for h in range(groups)
    )

    def own_rows(t):
        loads[t].wait()
        for copy in pack_copies[t]:
            copy.wait_recv()
        picked = jnp.zeros((rows, width), F32)
        for g in range(groups):
            keep = kept[:, g * tok:(g + 1) * tok]
            place = jnp.where((row_at == g * tok + col_at) & (keep > 0), 1.0, 0.0).astype(BF16)
            picked = picked + dot(place, inbox[g, t], (1, 0))
        xall[0, z, t] = picked.astype(BF16)

    def to_other(t, at, source):
        return remote(xall.at[0, source, t], xall.at[1, source, t], y_sems, t * 2 * zs + at, (me, other))

    def up(t, hop, source):
        return remote(
            xall.at[0, source, t], xall.at[0, source, t], up_sems, t * zs + hop, (me, (z + 1) * PAIR + y)
        )

    def down(t, hop, source):
        return remote(
            xall.at[0, source, t], xall.at[0, source, t], down_sems, t * zs + hop, (me, (z - 1) * PAIR + y)
        )

    def send_own(t):
        pl.when(z < zs - 1)(lambda: up(t, 1, z).start())
        pl.when(z > 0)(lambda: down(t, 1, z).start())
        to_other(t, 0, z).start()

    def pass_on(t):
        for hop in range(1, zs):
            @pl.when(z >= hop)
            def _(hop=hop):
                up(t, hop, z - hop).wait_recv()
                if hop < zs - 1:
                    pl.when(z < zs - 1)(lambda: up(t, hop + 1, z - hop).start())
                to_other(t, hop, z - hop).start()

            @pl.when(z + hop < zs)
            def _(hop=hop):
                down(t, hop, z + hop).wait_recv()
                if hop < zs - 1:
                    pl.when(z > 0)(lambda: down(t, hop + 1, z + hop).start())
                to_other(t, zs + hop, z + hop).start()

    def arrivals(t, wait):
        wait(to_other(t, 0, z))
        for hop in range(1, zs):
            pl.when(z >= hop)(lambda: wait(to_other(t, hop, z - hop)))
            pl.when(z + hop < zs)(lambda: wait(to_other(t, zs + hop, z + hop)))

    def passed(t):
        for hop in range(1, zs):
            pl.when((z < zs - 1) & (z >= hop - 1))(lambda: up(t, hop, z - hop + 1).wait_send())
            pl.when((z > 0) & (z + hop - 1 < zs))(lambda: down(t, hop, z + hop - 1).wait_send())
        arrivals(t, lambda copy: copy.wait_send())

    def x_rows(side, first, kind):
        return xall[side, pl.ds(first, per_dot), kind].reshape(per_dot * rows, width)

    def each(body):
        def step(i, carry):
            body(i * per_dot)
            return carry

        lax.fori_loop(0, zs // per_dot, step, 0)

    def project(side, kind, low, high, target):
        def step(first):
            out = dot(x_rows(side, first, kind), weights[:, low * slc:high * slc], (1, 0))
            target[pl.ds(side * zs + first, per_dot)] = (
                out.astype(BF16).reshape(per_dot, rows, (high - low) * slc)
            )

        each(step)

    def send_parts(t, source, target):
        copies = [
            remote(source.at[pl.ds(p * share, share)], target.at[me], part_sems, t * groups + d, (p, ep))
            for d, p in grp_peers
        ]
        for copy in copies:
            copy.start()
        return copies

    held = pl.ds(me * share, share)

    def summed(copies, source, target):
        total = source[held].astype(F32)
        for d, copy in zip(range(1, groups), copies):
            copy.wait_recv()
            total = total + target[lax.rem(me + groups - d, groups)].astype(F32)
        return total

    def share_out(t, ref):
        copies = [
            remote(ref.at[held], ref.at[held], grad_sems, t * groups + d, (p, ep))
            for d, p in grp_peers
        ]
        for copy in copies:
            copy.start()
        return copies

    def only_served(value):
        if experts == 1:
            return value
        row = lax.broadcasted_iota(jnp.int32, value.shape, 1)
        expert = lax.div(slots(lax.div(row, tok), lax.rem(row, tok)), cap)
        return jnp.where(expert == lax.div(placement_ref[ep], split), value, 0.0)

    def rows_of(ref, side, first):
        return ref[pl.ds(side * zs + first, per_dot)].reshape(per_dot * rows, ref.shape[-1])

    def produce(side, kind, target):
        def step(first):
            source, low, high = ((hidden, 2, 3), (grads, 0, 2))[kind]
            out = dot(rows_of(source, side, first), weights[:, low * slc:high * slc], (1, 1))
            target[pl.ds(first, per_dot), kind] = out.astype(target.dtype).reshape(per_dot, rows, width)

        each(step)

    order = [lax.rem(z + d, zs) for d in list(range(1, zs)) + [0]]

    def send_across(t):
        copies = [
            remote(outrows.at[q, t], yin.at[q, t], yo_sems, t * zs + i, (me, other))
            for i, q in enumerate(order)
        ]
        for copy in copies:
            copy.start()
        return copies

    def send_along(t, copies):
        out = []
        for i, q in enumerate(order):
            copies[i].wait()
            total = mine[q, t].astype(F32) + yin[q, t].astype(F32)
            if i < zs - 1:
                outrows[q, t] = total.astype(BF16)
                copy = remote(
                    outrows.at[q, t], zin.at[z, t], zo_sems, t * zs + i + 1, (me, q * PAIR + y)
                )
                copy.start()
                out.append(copy)
            else:
                own[t] = total
        return out

    for t in range(2):
        own_rows(t)
        send_own(t)
    pass_on(0)
    for load in loads[2:]:
        load.wait()
    project(0, 0, 0, 2, part_gu)
    pass_on(1)
    arrivals(0, lambda copy: copy.wait_recv())
    project(1, 0, 0, 2, part_gu)
    gu_copies = send_parts(0, part_gu, in_gu)
    project(0, 1, 2, 3, part_h)

    gate_up = summed(gu_copies, part_gu, in_gu)
    gate, up_part = gate_up[:, :, 0:slc], gate_up[:, :, slc:2 * slc]
    sig = jax.nn.sigmoid(gate)
    activated = gate * sig
    hidden[held] = only_served(activated * up_part).astype(BF16)
    hidden_copies = share_out(0, hidden)

    arrivals(1, lambda copy: copy.wait_recv())
    project(1, 1, 2, 3, part_h)
    h_copies = send_parts(1, part_h, in_h)

    for copy in hidden_copies:
        copy.wait_recv()
    produce(1, 0, outrows)
    across_ahead = send_across(0)
    produce(0, 0, mine)

    hidden_grad = summed(h_copies, part_h, in_h)
    gate_grad = hidden_grad * up_part * sig * (1.0 + gate * (1.0 - sig))
    grads[held, :, 0:slc] = only_served(gate_grad).astype(BF16)
    grads[held, :, slc:2 * slc] = only_served(hidden_grad * activated).astype(BF16)
    grad_copies = share_out(1, grads)

    along_ahead = send_along(0, across_ahead)

    for copy in grad_copies:
        copy.wait_recv()
    produce(1, 1, outrows)
    across_back = send_across(1)
    produce(0, 1, mine)
    along_back = send_along(1, across_back)

    if blocks == PAIR * per_dot:
        def both_sides(ref):
            return ref[...].reshape(blocks * rows, ref.shape[-1])

        def all_rows(kind):
            return xall[:, :, kind].reshape(blocks * rows, width)

        acc[:, 0:2 * slc] = dot(all_rows(0), both_sides(grads), (0, 0))
        acc[:, 2 * slc:3 * slc] = dot(all_rows(1), both_sides(hidden), (0, 0))
    else:
        acc[...] = jnp.zeros_like(acc)
        for side in range(PAIR):
            def step(first, side=side):
                acc[:, 0:2 * slc] += dot(x_rows(side, first, 0), rows_of(grads, side, first), (0, 0))
                acc[:, 2 * slc:3 * slc] += dot(x_rows(side, first, 1), rows_of(hidden, side, first), (0, 0))

            each(step)
    for i in range(3):
        grads_out[i] = acc[:, i * slc:(i + 1) * slc].astype(grads_out.dtype)

    target = dest * (fold * 2 * tok) + base
    picks = [
        jnp.where(out_at == target + f * 2 * tok, 1.0, 0.0).astype(BF16) for f in range(fold)
    ]
    for t, copies in enumerate((along_ahead, along_back)):
        for d, copy in zip(range(1, zs), copies):
            copy.wait_recv()
            own[t] += zin[lax.rem(z + zs - d, zs), t].astype(F32)

    final = own[...].astype(BF16).reshape(n_rows, width)
    placed = sum(dot(picks[f], final[:, f * cols:(f + 1) * cols], (1, 0)) for f in range(fold))
    outbox[...] = placed.astype(BF16).reshape(outbox.shape)
    out_copies = [remote(outbox.at[p], inbox2.at[me], out_sems, d, (p, ep)) for d, p in grp_peers]
    for copy in out_copies:
        copy.start()
    sent += out_copies + along_ahead + along_back + gu_copies + h_copies + hidden_copies + grad_copies
    inbox2[me] = outbox[me]
    for copy in out_copies:
        copy.wait_recv()
    rows_out[...] = inbox2[...]
    for copy in sent:
        copy.wait_send()
    passed(0)
    passed(1)


def body(tokens, cotangent, counts, destination, placement, gate_up_weight, down_weight):
    groups = lax.axis_size("grp")
    owners = lax.axis_size("ep")
    tok, model = tokens.shape[1], tokens.shape[2]
    experts = counts.shape[2]
    split = owners // experts
    width, slc = down_weight.shape[1], down_weight.shape[2]
    zs = owners // PAIR
    fold = max(1, 16 // (2 * tok))
    cols = width // fold
    box = fold * 2 * tok
    rows = groups * tok
    per_dot = min(zs, max(1, 64 // rows))
    lanes = -(-2 * rows // 128) * 128
    if width % 128:
        tokens, cotangent = (
            jnp.transpose(v[0].reshape(tok, groups, width), (1, 0, 2)) for v in (tokens, cotangent)
        )

    blocks = PAIR * zs
    share = blocks // groups
    vmem = pl.BlockSpec(memory_space=pltpu.VMEM)
    smem = pl.BlockSpec(memory_space=pltpu.SMEM)
    anywhere = pl.BlockSpec(memory_space=pl.ANY)
    shapes = [
        ((groups, 2, tok, width), BF16),
        ((groups, 8, lanes), jnp.int32),
        ((PAIR, zs, 2, rows, width), BF16),
        ((width, 3 * slc), BF16),
        ((blocks, rows, 2 * slc), BF16),
        ((blocks, rows, slc), BF16),
        ((groups, share, rows, 2 * slc), BF16),
        ((groups, share, rows, slc), BF16),
        ((blocks, rows, slc), BF16),
        ((blocks, rows, 2 * slc), BF16),
        ((zs, 2, rows, width), BF16),
        ((zs, 2, rows, width), F32 if zs * rows * width < (1 << 20) else BF16),
        ((zs, 2, rows, width), BF16),
        ((zs, 2, rows, width), BF16),
        ((2, rows, width), F32),
        ((groups, box, cols), BF16),
        ((groups, box, cols), BF16),
        ((width, 3 * slc), F32),
    ]
    dma = pltpu.SemaphoreType.DMA
    out, grads = pl.pallas_call(
        functools.partial(kernel, (groups, zs, fold, tok, experts, split, per_dot)),
        out_shape=(
            jax.ShapeDtypeStruct((groups, box, cols), BF16),
            jax.ShapeDtypeStruct((3, width, slc), BF16),
        ),
        in_specs=[anywhere, anywhere, smem, smem, smem, anywhere, anywhere],
        out_specs=(vmem, vmem),
        scratch_shapes=[pltpu.VMEM(s, t) for s, t in shapes] + [
            dma((2, 2 * groups)), dma((2, groups)), dma((2, 2 * zs)), dma((2, 2 * zs)), dma((2, 4 * zs)),
            dma((2, 2 * groups)), dma((2, 2 * groups)), dma((2, 2 * zs)), dma((2, 2 * zs)), dma((2, groups)),
            dma((5,)), dma((2,)),
        ],
        compiler_params=pltpu.CompilerParams(
            collective_id=0, has_side_effects=True, vmem_limit_bytes=60 << 20
        ),
    )(tokens, cotangent, destination, counts, placement, gate_up_weight[0], down_weight[0])
    out = out.reshape(groups, fold, 2, tok, cols)
    out = jnp.transpose(out, (2, 3, 0, 1, 4)).reshape(2, 1, tok, model)
    grads = grads.astype(F32)
    return out[0], out[1], grads[None, 0:2], grads[2:3]


def solution(mesh):
    return jax.shard_map(
        body,
        mesh=mesh,
        in_specs=(
            P("grp", "ep", None),
            P("grp", "ep", None),
            P("grp", "ep", None),
            P("grp", "ep", None),
            P(),
            P("ep", None, "grp", None),
            P("ep", "grp", None),
        ),
        out_specs=(
            P("grp", "ep", None),
            P("grp", "ep", None),
            P("ep", None, "grp", None),
            P("ep", "grp", None),
        ),
        check_vma=False,
    )
```

```python
import functools

import jax
import jax.numpy as jnp
import numpy as np
from jax import lax
from jax.experimental import pallas as pl
from jax.experimental.pallas import tpu as pltpu
from jax.sharding import PartitionSpec as P

MESH = pl.DeviceIdType.MESH
BF16 = jnp.bfloat16
F32 = jnp.float32
PAIR = 2


def dot(a, b, contract):
    return lax.dot_general(a, b, ((contract[:1], contract[1:]), ((), ())), preferred_element_type=F32)


def kernel(
    dims,
    tokens_ref, cotangent_ref, dest_ref, counts_ref, placement_ref, gate_up_ref, down_ref,
    rows_out, gate_up_out, down_out,
    inbox, metas, dests, xall, weights, part_gu, part_h, in_gu, in_h, hidden, grads, outrows, mine, yin, placed, zin, acc,
    pack_sems, meta_sems, dest_sems, z_sems, y_sems, part_sems, grad_sems, yo_sems, zo_sems, w_sems,
):
    groups, zs, tok, experts, split, per_dot = dims
    if len(outrows.shape) == 5:
        placed = outrows
    me, ep = lax.axis_index("grp"), lax.axis_index("ep")
    z, y = ep // PAIR, ep % PAIR
    other = z * PAIR + (PAIR - 1 - y)
    width, slc = xall.shape[-1], hidden.shape[-1]
    rows = xall.shape[3]
    block, cap = tok // groups, tok // experts
    blocks = PAIR * zs
    share = blocks // groups
    n_rows = 2 * rows

    grp_peers = [(d, lax.rem(me + d, groups)) for d in range(1, groups)]
    z_peers = [(d, lax.rem(z + d, zs)) for d in range(1, zs)]

    def for_groups(first, body):
        if groups <= 8:
            for d in range(first, groups):
                body(d)
        else:
            def step(d, carry):
                body(d)
                return carry

            lax.fori_loop(first, groups, step, 0)

    order = [(i, lax.rem(z + i + 1, zs)) for i in range(zs)]

    barrier = pltpu.get_barrier_semaphore()
    for i, q in order:
        def greet(d, q=q):
            pl.semaphore_signal(
                barrier, inc=1, device_id=(lax.rem(me + d, groups), q * PAIR + y), device_id_type=MESH
            )

        for_groups(1 if i == zs - 1 else 0, greet)
    pl.semaphore_signal(barrier, inc=1, device_id=(me, other), device_id_type=MESH)

    def piece(ref, p):
        if ref.shape[0] == 1:
            return ref.at[0, :, pl.ds(pl.multiple_of(p * width, width), width)]
        return ref.at[p]

    loads = [
        pltpu.make_async_copy(piece(tokens_ref, me), inbox.at[me, 0], w_sems.at[3]),
        pltpu.make_async_copy(piece(cotangent_ref, me), inbox.at[me, 1], w_sems.at[4]),
        pltpu.make_async_copy(gate_up_ref.at[0], weights.at[:, pl.ds(0, slc)], w_sems.at[0]),
        pltpu.make_async_copy(gate_up_ref.at[1], weights.at[:, pl.ds(slc, slc)], w_sems.at[1]),
        pltpu.make_async_copy(down_ref, weights.at[:, pl.ds(2 * slc, slc)], w_sems.at[2]),
    ]
    for load in loads:
        load.start()

    lanes = metas.shape[-1]
    lane = lax.broadcasted_iota(jnp.int32, (8, lanes), 1)
    line = lax.broadcasted_iota(jnp.int32, (8, lanes), 0)

    def slots(group, row):
        return group * block + lax.rem(row, block)

    lane_row, lane_group = lax.rem(lane, tok), lax.rem(lax.div(lane, tok), groups)
    lane_block = lax.div(lane_row, block)
    lane_expert = lax.div(slots(lane_group, lane_row), cap)
    own_dest = sum(jnp.where(lane_block == b, dest_ref[0, 0, b], 0) for b in range(groups))
    own_count = sum(jnp.where(lane_expert == e, counts_ref[0, 0, e], 0) for e in range(experts))
    metas[me] = jnp.where(line == 0, own_dest, own_count)

    pl.semaphore_wait(barrier, groups * zs)

    def remote(src, dst, sems, at, device):
        return pltpu.make_async_remote_copy(
            src_ref=src, dst_ref=dst, send_sem=sems.at[0, at], recv_sem=sems.at[1, at],
            device_id=device, device_id_type=MESH,
        )

    sent = []

    meta_copies = [remote(metas.at[me], metas.at[me], meta_sems, d, (p, ep)) for d, p in grp_peers]
    pack_copies = [
        [
            remote(piece(ref, p), inbox.at[me, t], pack_sems, t * groups + d, (p, ep))
            for d, p in grp_peers
        ]
        for t, ref in enumerate((tokens_ref, cotangent_ref))
    ]
    for copy in meta_copies + pack_copies[0] + pack_copies[1]:
        copy.start()
    sent += meta_copies + pack_copies[0] + pack_copies[1]

    m = lax.broadcasted_iota(jnp.int32, (1, n_rows), 1)
    m_group, m_row = lax.rem(lax.div(m, tok), groups), lax.rem(m, tok)
    slot = slots(m_group, m_row)
    row_at = lax.broadcasted_iota(jnp.int32, (rows, tok), 0)
    col_at = lax.broadcasted_iota(jnp.int32, (rows, tok), 1)

    for copy in meta_copies:
        copy.wait_recv()
    dest = sum(jnp.where(m_group == g, metas[g, 0:1, 0:n_rows], 0) for g in range(groups))
    kept = sum(
        jnp.where((dest == h) & (lax.rem(slot, cap) < metas[h, 1:2, 0:n_rows]), 1, 0)
        for h in range(groups)
    )
    dests[z, :, 0:n_rows] = jnp.broadcast_to(dest, (8, n_rows))
    dest_copies = [remote(dests.at[z], dests.at[z], dest_sems, d, (me, q * PAIR + y)) for d, q in z_peers]
    for copy in dest_copies:
        copy.start()
    sent += dest_copies

    def own_rows(t):
        loads[t].wait()
        for copy in pack_copies[t]:
            copy.wait_recv()
        picked = jnp.zeros((rows, width), F32)
        for g in range(groups):
            keep = kept[:, g * tok:(g + 1) * tok]
            place = jnp.where((row_at == g * tok + col_at) & (keep > 0), 1.0, 0.0).astype(BF16)
            picked = picked + dot(place, inbox[g, t], (1, 0))
        xall[0, z, t] = picked.astype(BF16)

    def to_other(t, at, source):
        return remote(xall.at[0, source, t], xall.at[1, source, t], y_sems, t * zs + at, (me, other))

    def along(t, d):
        return remote(
            xall.at[0, z, t], xall.at[0, z, t], z_sems, t * zs + d, (me, lax.rem(z + d, zs) * PAIR + y)
        )

    def send_own(t):
        to_other(t, 0, z).start()
        for d in range(1, zs):
            along(t, d).start()

    def pass_on(t):
        for d in range(1, zs):
            along(t, d).wait_recv()
            to_other(t, d, lax.rem(z + zs - d, zs)).start()

    def arrivals(t):
        for d in range(zs):
            to_other(t, d, lax.rem(z + zs - d, zs)).wait_recv()

    def passed(t):
        for d in range(zs):
            if d > 0:
                along(t, d).wait_send()
            to_other(t, d, lax.rem(z + zs - d, zs)).wait_send()

    def x_rows(side, first, kind):
        return xall[side, pl.ds(first, per_dot), kind].reshape(per_dot * rows, width)

    def each(body):
        def step(i, carry):
            body(i * per_dot)
            return carry

        lax.fori_loop(0, zs // per_dot, step, 0)

    def project(side, kind, low, high, target):
        def step(first):
            out = dot(x_rows(side, first, kind), weights[:, low * slc:high * slc], (1, 0))
            target[pl.ds(side * zs + first, per_dot)] = (
                out.astype(BF16).reshape(per_dot, rows, (high - low) * slc)
            )

        each(step)

    def send_parts(t, source, target):
        copies = [
            remote(source.at[pl.ds(p * share, share)], target.at[me], part_sems, t * groups + d, (p, ep))
            for d, p in grp_peers
        ]
        for copy in copies:
            copy.start()
        return copies

    held = pl.ds(me * share, share)

    def summed(copies, source, target):
        total = source[held].astype(F32)
        for d, copy in zip(range(1, groups), copies):
            copy.wait_recv()
            total = total + target[lax.rem(me + groups - d, groups)].astype(F32)
        return total

    def share_out(t, ref):
        copies = [
            remote(ref.at[held], ref.at[held], grad_sems, t * groups + d, (p, ep))
            for d, p in grp_peers
        ]
        for copy in copies:
            copy.start()
        return copies

    def only_served(value):
        if experts == 1:
            return value
        row = lax.broadcasted_iota(jnp.int32, value.shape, 1)
        expert = lax.div(slots(lax.div(row, tok), lax.rem(row, tok)), cap)
        return jnp.where(expert == lax.div(placement_ref[ep], split), value, 0.0)

    def rows_of(ref, side, first):
        return ref[pl.ds(side * zs + first, per_dot)].reshape(per_dot * rows, ref.shape[-1])

    def produce(side, kind, target):
        def step(first):
            source, low, high = ((hidden, 2, 3), (grads, 0, 2))[kind]
            out = dot(rows_of(source, side, first), weights[:, low * slc:high * slc], (1, 1))
            target[pl.ds(first, per_dot), kind] = out.astype(target.dtype).reshape((per_dot,) + target.shape[2:])

        each(step)

    def send_across(t):
        copies = [
            remote(outrows.at[q, t], yin.at[q, t], yo_sems, t * zs + i, (me, other)) for i, q in order
        ]
        for copy in copies:
            copy.start()
        return copies

    def deliver(t, i, q, d):
        p = lax.rem(me + d, groups)
        return remote(
            placed.at[q, t, p], zin.at[z, me, t], zo_sems, (t * zs + i) * groups + d, (p, q * PAIR + y)
        )

    slot_at = lax.broadcasted_iota(jnp.int32, (tok, rows), 0)

    def send_home(t, copies):
        for i, q in order:
            copies[i].wait()
            total = (mine[q, t].astype(F32) + yin[q, t].reshape(rows, width).astype(F32)).astype(BF16)
            going = dests[q, 0:1, 0:rows]

            def place(p):
                pick = jnp.where((slot_at == slot[:, 0:rows]) & (going == p), 1.0, 0.0).astype(BF16)
                return dot(pick, total, (1, 0)).astype(BF16)

            def send(d, i=i, q=q, place=place):
                p = lax.rem(me + d, groups)
                placed[q, t, p] = place(p)
                deliver(t, i, q, d).start()

            for_groups(1 if i == zs - 1 else 0, send)
            if i == zs - 1:
                zin[z, me, t] = place(me)

    def delivered(t, wait):
        for i, q in order:
            for_groups(1 if i == zs - 1 else 0, lambda d, i=i, q=q: wait(deliver(t, i, q, d)))

    for t in range(2):
        own_rows(t)
        send_own(t)
    pass_on(0)
    for load in loads[2:]:
        load.wait()
    project(0, 0, 0, 2, part_gu)
    pass_on(1)
    arrivals(0)
    project(1, 0, 0, 2, part_gu)
    gu_copies = send_parts(0, part_gu, in_gu)
    project(0, 1, 2, 3, part_h)

    gate_up = summed(gu_copies, part_gu, in_gu)
    gate, up_part = gate_up[:, :, 0:slc], gate_up[:, :, slc:2 * slc]
    sig = jax.nn.sigmoid(gate)
    activated = gate * sig
    hidden[held] = only_served(activated * up_part).astype(BF16)
    hidden_copies = share_out(0, hidden)

    arrivals(1)
    project(1, 1, 2, 3, part_h)
    h_copies = send_parts(1, part_h, in_h)

    for copy in hidden_copies:
        copy.wait_recv()
    produce(1, 0, outrows)
    across_ahead = send_across(0)
    produce(0, 0, mine)

    hidden_grad = summed(h_copies, part_h, in_h)
    gate_grad = hidden_grad * up_part * sig * (1.0 + gate * (1.0 - sig))
    grads[held, :, 0:slc] = only_served(gate_grad).astype(BF16)
    grads[held, :, slc:2 * slc] = only_served(hidden_grad * activated).astype(BF16)
    grad_copies = share_out(1, grads)

    for copy in dest_copies:
        copy.wait_recv()
    send_home(0, across_ahead)

    for copy in grad_copies:
        copy.wait_recv()
    produce(1, 1, outrows)
    across_back = send_across(1)
    produce(0, 1, mine)
    send_home(1, across_back)

    if blocks == PAIR * per_dot:
        def both_sides(ref):
            return ref[...].reshape(blocks * rows, ref.shape[-1])

        def all_rows(kind):
            return xall[:, :, kind].reshape(blocks * rows, width)

        acc[:, 0:2 * slc] = dot(all_rows(0), both_sides(grads), (0, 0))
        acc[:, 2 * slc:3 * slc] = dot(all_rows(1), both_sides(hidden), (0, 0))
    else:
        acc[...] = jnp.zeros_like(acc)
        for side in range(PAIR):
            def step(first, side=side):
                acc[:, 0:2 * slc] += dot(x_rows(side, first, 0), rows_of(grads, side, first), (0, 0))
                acc[:, 2 * slc:3 * slc] += dot(x_rows(side, first, 1), rows_of(hidden, side, first), (0, 0))

            each(step)
    for i in range(2):
        gate_up_out[i] = acc[:, i * slc:(i + 1) * slc].astype(gate_up_out.dtype)
    down_out[...] = acc[:, 2 * slc:3 * slc].astype(down_out.dtype)

    for t in range(2):
        delivered(t, lambda copy: copy.wait_recv())
        for g in range(groups):
            total = zin[0, g, t].astype(F32)
            for q in range(1, zs):
                total = total + zin[q, g, t].astype(F32)
            total = total.astype(BF16)
            if rows_out.shape[0] == 2:
                rows_out[t, :, g * width:(g + 1) * width] = total
            else:
                rows_out[g, t] = total
    sent += gu_copies + h_copies + hidden_copies + grad_copies
    for copy in sent:
        copy.wait_send()
    for t in range(2):
        passed(t)
        delivered(t, lambda copy: copy.wait_send())


def body(tokens, cotangent, counts, destination, placement, gate_up_weight, down_weight):
    groups = lax.axis_size("grp")
    owners = lax.axis_size("ep")
    tok, model = tokens.shape[1], tokens.shape[2]
    experts = counts.shape[2]
    split = owners // experts
    width, slc = down_weight.shape[1], down_weight.shape[2]
    zs = owners // PAIR
    rows = groups * tok
    per_dot = min(zs, max(1, 64 // rows))
    lanes = -(-2 * rows // 128) * 128
    if width % 128:
        tokens, cotangent = (
            jnp.transpose(v[0].reshape(tok, groups, width), (1, 0, 2)) for v in (tokens, cotangent)
        )

    blocks = PAIR * zs
    share = blocks // groups
    vmem = pl.BlockSpec(memory_space=pltpu.VMEM)
    smem = pl.BlockSpec(memory_space=pltpu.SMEM)
    anywhere = pl.BlockSpec(memory_space=pl.ANY)
    large = zs * rows * width >= (1 << 20)
    flat = (groups, tok, width) if large else (rows, width)
    shapes = [
        ((groups, 2, tok, width), BF16),
        ((groups, 8, lanes), jnp.int32),
        ((zs, 8, lanes), jnp.int32),
        ((PAIR, zs, 2, rows, width), BF16),
        ((width, 3 * slc), BF16),
        ((blocks, rows, 2 * slc), BF16),
        ((blocks, rows, slc), BF16),
        ((groups, share, rows, 2 * slc), BF16),
        ((groups, share, rows, slc), BF16),
        ((blocks, rows, slc), BF16),
        ((blocks, rows, 2 * slc), BF16),
        ((zs, 2) + flat, BF16),
        ((zs, 2, rows, width), BF16 if large else F32),
        ((zs, 2) + flat, BF16),
        ((1, 1, 1, tok, width) if large else (zs, 2, groups, tok, width), BF16),
        ((zs, groups, 2, tok, width), BF16),
        ((width, 3 * slc), F32),
    ]
    dma = pltpu.SemaphoreType.DMA
    out, gate_up_grad, down_grad = pl.pallas_call(
        functools.partial(kernel, (groups, zs, tok, experts, split, per_dot)),
        out_shape=(
            jax.ShapeDtypeStruct((groups, 2, tok, width) if width % 128 else (2, tok, model), BF16),
            jax.ShapeDtypeStruct((2, width, slc), BF16),
            jax.ShapeDtypeStruct((width, slc), BF16),
        ),
        in_specs=[anywhere, anywhere, smem, smem, smem, anywhere, anywhere],
        out_specs=(vmem, vmem, vmem),
        scratch_shapes=[pltpu.VMEM(s, t) for s, t in shapes] + [
            dma((2, 2 * groups)), dma((2, groups)), dma((2, zs)), dma((2, 2 * zs)), dma((2, 2 * zs)),
            dma((2, 2 * groups)), dma((2, 2 * groups)), dma((2, 2 * zs)), dma((2, 2 * zs * groups)), dma((5,)),
        ],
        compiler_params=pltpu.CompilerParams(
            collective_id=0, has_side_effects=True, vmem_limit_bytes=60 << 20
        ),
    )(tokens, cotangent, destination, counts, placement, gate_up_weight[0], down_weight[0])
    if width % 128:
        out = jnp.transpose(out, (1, 2, 0, 3)).reshape(2, tok, model)
    return out[0:1], out[1:2], gate_up_grad[None].astype(F32), down_grad[None].astype(F32)


def solution(mesh):
    return jax.shard_map(
        body,
        mesh=mesh,
        in_specs=(
            P("grp", "ep", None),
            P("grp", "ep", None),
            P("grp", "ep", None),
            P("grp", "ep", None),
            P(),
            P("ep", None, "grp", None),
            P("ep", "grp", None),
        ),
        out_specs=(
            P("grp", "ep", None),
            P("grp", "ep", None),
            P("ep", None, "grp", None),
            P("ep", "grp", None),
        ),
        check_vma=False,
    )
```

```python
import functools

import jax
import jax.numpy as jnp
import numpy as np
from jax import lax
from jax.experimental import pallas as pl
from jax.experimental.pallas import tpu as pltpu
from jax.sharding import PartitionSpec as P

MESH = pl.DeviceIdType.MESH
BF16 = jnp.bfloat16
F32 = jnp.float32
PAIR = 2


def dot(a, b, contract):
    return lax.dot_general(a, b, ((contract[:1], contract[1:]), ((), ())), preferred_element_type=F32)


def kernel(
    dims,
    tokens_ref, cotangent_ref, dest_ref, counts_ref, placement_ref, gate_up_ref, down_ref,
    rows_out, gate_up_out, down_out,
    inbox, metas, xall, weights, turned, part_gu, part_h, in_gu, in_h, hidden, grads, outrows, mine, yin, placed, zin, acc,
    pack_sems, meta_sems, z_sems, y_sems, part_sems, grad_sems, yo_sems, zo_sems, w_sems,
):
    groups, zs, tok, experts, split, per_dot = dims
    if len(outrows.shape) == 5:
        placed = outrows
    me, ep = lax.axis_index("grp"), lax.axis_index("ep")
    z, y = ep // PAIR, ep % PAIR
    other = z * PAIR + (PAIR - 1 - y)
    width, slc = xall.shape[-1], hidden.shape[-1]
    rows = xall.shape[3]
    block, cap = tok // groups, tok // experts
    blocks = PAIR * zs
    share = blocks // groups
    n_rows = 2 * rows

    grp_peers = [(d, lax.rem(me + d, groups)) for d in range(1, groups)]
    z_peers = [(d, lax.rem(z + d, zs)) for d in range(1, zs)]

    def for_groups(first, body):
        if groups <= 8:
            for d in range(first, groups):
                body(d)
        else:
            def step(d, carry):
                body(d)
                return carry

            lax.fori_loop(first, groups, step, 0)

    order = [(i, lax.rem(z + i + 1, zs)) for i in range(zs)]

    barrier = pltpu.get_barrier_semaphore()
    for i, q in order:
        def greet(d, q=q):
            pl.semaphore_signal(
                barrier, inc=1, device_id=(lax.rem(me + d, groups), q * PAIR + y), device_id_type=MESH
            )

        for_groups(1 if i == zs - 1 else 0, greet)
    pl.semaphore_signal(barrier, inc=1, device_id=(me, other), device_id_type=MESH)

    def piece(ref, p):
        if ref.shape[0] == 1:
            return ref.at[0, :, pl.ds(pl.multiple_of(p * width, width), width)]
        return ref.at[p]

    loads = [
        pltpu.make_async_copy(piece(tokens_ref, me), inbox.at[me, 0], w_sems.at[3]),
        pltpu.make_async_copy(piece(cotangent_ref, me), inbox.at[me, 1], w_sems.at[4]),
        pltpu.make_async_copy(gate_up_ref.at[0], weights.at[:, pl.ds(0, slc)], w_sems.at[0]),
        pltpu.make_async_copy(gate_up_ref.at[1], weights.at[:, pl.ds(slc, slc)], w_sems.at[1]),
        pltpu.make_async_copy(down_ref, weights.at[:, pl.ds(2 * slc, slc)], w_sems.at[2]),
    ]
    for load in loads:
        load.start()

    lanes = metas.shape[-1]
    lane = lax.broadcasted_iota(jnp.int32, (8, lanes), 1)
    line = lax.broadcasted_iota(jnp.int32, (8, lanes), 0)

    def slots(group, row):
        return group * block + lax.rem(row, block)

    lane_row, lane_group = lax.rem(lane, tok), lax.rem(lax.div(lane, tok), groups)
    lane_block = lax.div(lane_row, block)
    lane_expert = lax.div(slots(lane_group, lane_row), cap)
    own_dest = sum(jnp.where(lane_block == b, dest_ref[0, 0, b], 0) for b in range(groups))
    own_count = sum(jnp.where(lane_expert == e, counts_ref[0, 0, e], 0) for e in range(experts))
    metas[me] = jnp.where(line == 0, own_dest, own_count)

    pl.semaphore_wait(barrier, groups * zs)

    def remote(src, dst, sems, at, device):
        return pltpu.make_async_remote_copy(
            src_ref=src, dst_ref=dst, send_sem=sems.at[0, at], recv_sem=sems.at[1, at],
            device_id=device, device_id_type=MESH,
        )

    sent = []

    meta_copies = [remote(metas.at[me], metas.at[me], meta_sems, d, (p, ep)) for d, p in grp_peers]
    pack_copies = [
        [
            remote(piece(ref, p), inbox.at[me, t], pack_sems, t * groups + d, (p, ep))
            for d, p in grp_peers
        ]
        for t, ref in enumerate((tokens_ref, cotangent_ref))
    ]
    for copy in meta_copies + pack_copies[0] + pack_copies[1]:
        copy.start()
    sent += meta_copies + pack_copies[0] + pack_copies[1]

    m = lax.broadcasted_iota(jnp.int32, (1, n_rows), 1)
    m_group, m_row = lax.rem(lax.div(m, tok), groups), lax.rem(m, tok)
    slot = slots(m_group, m_row)
    row_at = lax.broadcasted_iota(jnp.int32, (rows, tok), 0)

    for copy in meta_copies:
        copy.wait_recv()
    dest = sum(jnp.where(m_group == g, metas[g, 0:1, 0:n_rows], 0) for g in range(groups))
    kept = sum(
        jnp.where((dest == h) & (lax.rem(slot, cap) < metas[h, 1:2, 0:n_rows]), 1, 0)
        for h in range(groups)
    )
    home = jnp.where(kept > 0, dest * tok + slot, -1)

    def own_rows(t):
        loads[t].wait()
        for copy in pack_copies[t]:
            copy.wait_recv()
        picked = jnp.zeros((rows, width), F32)
        for g in range(groups):
            place = jnp.where(row_at == home[:, g * tok:(g + 1) * tok], 1.0, 0.0).astype(BF16)
            picked = picked + dot(place, inbox[g, t], (1, 0))
        xall[0, z, t] = picked.astype(BF16)

    def to_other(t, at, source):
        return remote(xall.at[0, source, t], xall.at[1, source, t], y_sems, t * zs + at, (me, other))

    def along(t, d):
        return remote(
            xall.at[0, z, t], xall.at[0, z, t], z_sems, t * zs + d, (me, lax.rem(z + d, zs) * PAIR + y)
        )

    def send_own(t):
        to_other(t, 0, z).start()
        for d in range(1, zs):
            along(t, d).start()

    def pass_on(t):
        for d in range(1, zs):
            along(t, d).wait_recv()
            to_other(t, d, lax.rem(z + zs - d, zs)).start()

    def arrivals(t):
        for d in range(zs):
            to_other(t, d, lax.rem(z + zs - d, zs)).wait_recv()

    def passed(t):
        for d in range(zs):
            if d > 0:
                along(t, d).wait_send()
            to_other(t, d, lax.rem(z + zs - d, zs)).wait_send()

    def x_rows(side, first, kind):
        return xall[side, pl.ds(first, per_dot), kind].reshape(per_dot * rows, width)

    def each(body):
        def step(i, carry):
            body(i * per_dot)
            return carry

        lax.fori_loop(0, zs // per_dot, step, 0)

    def project(side, kind, low, high, target):
        def step(first):
            out = dot(x_rows(side, first, kind), weights[:, low * slc:high * slc], (1, 0))
            target[pl.ds(side * zs + first, per_dot)] = (
                out.astype(BF16).reshape(per_dot, rows, (high - low) * slc)
            )

        each(step)

    def send_parts(t, source, target):
        copies = [
            remote(source.at[pl.ds(p * share, share)], target.at[me], part_sems, t * groups + d, (p, ep))
            for d, p in grp_peers
        ]
        for copy in copies:
            copy.start()
        return copies

    held = pl.ds(me * share, share)

    def summed(copies, source, target):
        total = source[held].astype(F32)
        for d, copy in zip(range(1, groups), copies):
            copy.wait_recv()
            total = total + target[lax.rem(me + groups - d, groups)].astype(F32)
        return total

    def share_out(t, ref):
        copies = [
            remote(ref.at[held], ref.at[held], grad_sems, t * groups + d, (p, ep))
            for d, p in grp_peers
        ]
        for copy in copies:
            copy.start()
        return copies

    def only_served(value):
        if experts == 1:
            return value
        row = lax.broadcasted_iota(jnp.int32, value.shape, 1)
        expert = lax.div(lax.rem(row, tok), cap)
        return jnp.where(expert == lax.div(placement_ref[ep], split), value, 0.0)

    def rows_of(ref, side, first):
        return ref[pl.ds(side * zs + first, per_dot)].reshape(per_dot * rows, ref.shape[-1])

    def produce(side, kind, target):
        def step(first):
            source, low, high = ((hidden, 2, 3), (grads, 0, 2))[kind]
            out = dot(rows_of(source, side, first), turned[low * slc:high * slc, :], (1, 0))
            target[pl.ds(first, per_dot), kind] = out.astype(target.dtype).reshape((per_dot,) + target.shape[2:])

        each(step)

    def send_across(t):
        copies = [
            remote(outrows.at[q, t], yin.at[q, t], yo_sems, t * zs + i, (me, other)) for i, q in order
        ]
        for copy in copies:
            copy.start()
        return copies

    def deliver(t, i, q, d):
        p = lax.rem(me + d, groups)
        return remote(
            placed.at[q, t, p], zin.at[z, me, t], zo_sems, (t * zs + i) * groups + d, (p, q * PAIR + y)
        )

    def send_home(t, copies):
        for i, q in order:
            copies[i].wait()
            total = mine[q, t].astype(F32) + yin[q, t].reshape(rows, width).astype(F32)
            for p in range(groups):
                placed[q, t, p] = total[p * tok:(p + 1) * tok].astype(BF16)

            def send(d, i=i, q=q):
                deliver(t, i, q, d).start()

            for_groups(1 if i == zs - 1 else 0, send)
            if i == zs - 1:
                zin[z, me, t] = placed[q, t, me]

    def delivered(t, wait):
        for i, q in order:
            for_groups(1 if i == zs - 1 else 0, lambda d, i=i, q=q: wait(deliver(t, i, q, d)))

    for t in range(2):
        own_rows(t)
        send_own(t)
    for load in loads[2:]:
        load.wait()
    turned[...] = jnp.transpose(weights[...], (1, 0))
    pass_on(0)
    project(0, 0, 0, 2, part_gu)
    pass_on(1)
    arrivals(0)
    project(1, 0, 0, 2, part_gu)
    gu_copies = send_parts(0, part_gu, in_gu)
    project(0, 1, 2, 3, part_h)

    gate_up = summed(gu_copies, part_gu, in_gu)
    gate, up_part = gate_up[:, :, 0:slc], gate_up[:, :, slc:2 * slc]
    sig = jax.nn.sigmoid(gate)
    activated = gate * sig
    hidden[held] = only_served(activated * up_part).astype(BF16)
    hidden_copies = share_out(0, hidden)

    arrivals(1)
    project(1, 1, 2, 3, part_h)
    h_copies = send_parts(1, part_h, in_h)

    for copy in hidden_copies:
        copy.wait_recv()
    produce(1, 0, outrows)
    across_ahead = send_across(0)
    produce(0, 0, mine)

    hidden_grad = summed(h_copies, part_h, in_h)
    gate_grad = hidden_grad * up_part * sig * (1.0 + gate * (1.0 - sig))
    grads[held, :, 0:slc] = only_served(gate_grad).astype(BF16)
    grads[held, :, slc:2 * slc] = only_served(hidden_grad * activated).astype(BF16)
    grad_copies = share_out(1, grads)

    send_home(0, across_ahead)

    for copy in grad_copies:
        copy.wait_recv()
    produce(1, 1, outrows)
    across_back = send_across(1)
    produce(0, 1, mine)
    send_home(1, across_back)

    if blocks == PAIR * per_dot:
        def both_sides(ref):
            return ref[...].reshape(blocks * rows, ref.shape[-1])

        def all_rows(kind):
            return xall[:, :, kind].reshape(blocks * rows, width)

        acc[:, 0:2 * slc] = dot(all_rows(0), both_sides(grads), (0, 0))
        acc[:, 2 * slc:3 * slc] = dot(all_rows(1), both_sides(hidden), (0, 0))
    else:
        acc[...] = jnp.zeros_like(acc)
        for side in range(PAIR):
            def step(first, side=side):
                acc[:, 0:2 * slc] += dot(x_rows(side, first, 0), rows_of(grads, side, first), (0, 0))
                acc[:, 2 * slc:3 * slc] += dot(x_rows(side, first, 1), rows_of(hidden, side, first), (0, 0))

            each(step)
    for i in range(2):
        gate_up_out[i] = acc[:, i * slc:(i + 1) * slc].astype(gate_up_out.dtype)
    down_out[...] = acc[:, 2 * slc:3 * slc].astype(down_out.dtype)

    for t in range(2):
        delivered(t, lambda copy: copy.wait_recv())
        for g in range(groups):
            total = zin[0, g, t].astype(F32)
            for q in range(1, zs):
                total = total + zin[q, g, t].astype(F32)
            total = total.astype(BF16)
            if rows_out.shape[0] == 2:
                rows_out[t, :, g * width:(g + 1) * width] = total
            else:
                rows_out[g, t] = total
    sent += gu_copies + h_copies + hidden_copies + grad_copies
    for copy in sent:
        copy.wait_send()
    for t in range(2):
        passed(t)
        delivered(t, lambda copy: copy.wait_send())


def body(tokens, cotangent, counts, destination, placement, gate_up_weight, down_weight):
    groups = lax.axis_size("grp")
    owners = lax.axis_size("ep")
    tok, model = tokens.shape[1], tokens.shape[2]
    experts = counts.shape[2]
    split = owners // experts
    width, slc = down_weight.shape[1], down_weight.shape[2]
    zs = owners // PAIR
    rows = groups * tok
    per_dot = min(zs, max(1, 64 // rows))
    lanes = -(-2 * rows // 128) * 128
    if width % 128:
        tokens, cotangent = (
            jnp.transpose(v[0].reshape(tok, groups, width), (1, 0, 2)) for v in (tokens, cotangent)
        )

    blocks = PAIR * zs
    share = blocks // groups
    vmem = pl.BlockSpec(memory_space=pltpu.VMEM)
    smem = pl.BlockSpec(memory_space=pltpu.SMEM)
    hbm = pl.BlockSpec(memory_space=pltpu.HBM)
    large = zs * rows * width >= (1 << 20)
    flat = (groups, tok, width) if large else (rows, width)
    shapes = [
        ((groups, 2, tok, width), BF16),
        ((groups, 8, lanes), jnp.int32),
        ((PAIR, zs, 2, rows, width), BF16),
        ((width, 3 * slc), BF16),
        ((3 * slc, width), BF16),
        ((blocks, rows, 2 * slc), BF16),
        ((blocks, rows, slc), BF16),
        ((groups, share, rows, 2 * slc), BF16),
        ((groups, share, rows, slc), BF16),
        ((blocks, rows, slc), BF16),
        ((blocks, rows, 2 * slc), BF16),
        ((zs, 2) + flat, BF16),
        ((zs, 2, rows, width), BF16 if large else F32),
        ((zs, 2) + flat, BF16),
        ((1, 1, 1, tok, width) if large else (zs, 2, groups, tok, width), BF16),
        ((zs, groups, 2, tok, width), BF16),
        ((width, 3 * slc), F32),
    ]
    dma = pltpu.SemaphoreType.DMA
    out, gate_up_grad, down_grad = pl.pallas_call(
        functools.partial(kernel, (groups, zs, tok, experts, split, per_dot)),
        out_shape=(
            jax.ShapeDtypeStruct((groups, 2, tok, width) if width % 128 else (2, tok, model), BF16),
            jax.ShapeDtypeStruct((2, width, slc), BF16),
            jax.ShapeDtypeStruct((width, slc), BF16),
        ),
        in_specs=[hbm, hbm, smem, smem, smem, hbm, hbm],
        out_specs=(vmem, vmem, vmem),
        scratch_shapes=[pltpu.VMEM(s, t) for s, t in shapes] + [
            dma((2, 2 * groups)), dma((2, groups)), dma((2, 2 * zs)), dma((2, 2 * zs)),
            dma((2, 2 * groups)), dma((2, 2 * groups)), dma((2, 2 * zs)), dma((2, 2 * zs * groups)), dma((5,)),
        ],
        compiler_params=pltpu.CompilerParams(
            collective_id=0, has_side_effects=True, vmem_limit_bytes=60 << 20
        ),
    )(tokens, cotangent, destination, counts, placement, gate_up_weight[0], down_weight[0])
    if width % 128:
        out = jnp.transpose(out, (1, 2, 0, 3)).reshape(2, tok, model)
    return out[0:1], out[1:2], gate_up_grad[None].astype(F32), down_grad[None].astype(F32)


def solution(mesh):
    return jax.shard_map(
        body,
        mesh=mesh,
        in_specs=(
            P("grp", "ep", None),
            P("grp", "ep", None),
            P("grp", "ep", None),
            P("grp", "ep", None),
            P(),
            P("ep", None, "grp", None),
            P("ep", "grp", None),
        ),
        out_specs=(
            P("grp", "ep", None),
            P("grp", "ep", None),
            P("ep", None, "grp", None),
            P("ep", "grp", None),
        ),
        check_vma=False,
    )
```

```python
import functools

import jax
import jax.numpy as jnp
import numpy as np
from jax import lax
from jax.experimental import pallas as pl
from jax.experimental.pallas import tpu as pltpu
from jax.sharding import PartitionSpec as P

MESH = pl.DeviceIdType.MESH
BF16 = jnp.bfloat16
F32 = jnp.float32
PAIR = 2


def dot(a, b, contract):
    return lax.dot_general(a, b, ((contract[:1], contract[1:]), ((), ())), preferred_element_type=F32)


def kernel(
    dims,
    tokens_ref, cotangent_ref, dest_ref, counts_ref, placement_ref, gate_up_ref, down_ref,
    rows_out, gate_up_out, down_out,
    inbox, metas, xall, weights, turned, part_gu, part_h, in_gu, in_h, hidden, grads, outrows, mine, yin, placed, zin, acc, gate_up_held, down_held,
    pack_sems, meta_sems, z_sems, y_sems, part_sems, grad_sems, yo_sems, zo_sems, w_sems, o_sems,
):
    groups, zs, tok, experts, split, per_dot = dims
    if len(outrows.shape) == 5:
        placed = outrows
    me, ep = lax.axis_index("grp"), lax.axis_index("ep")
    z, y = ep // PAIR, ep % PAIR
    other = z * PAIR + (PAIR - 1 - y)
    width, slc = xall.shape[-1], hidden.shape[-1]
    rows = xall.shape[3]
    block, cap = tok // groups, tok // experts
    blocks = PAIR * zs
    share = blocks // groups
    n_rows = 2 * rows

    grp_peers = [(d, lax.rem(me + d, groups)) for d in range(1, groups)]
    z_peers = [(d, lax.rem(z + d, zs)) for d in range(1, zs)]

    def for_groups(first, body):
        if groups <= 8:
            for d in range(first, groups):
                body(d)
        else:
            def step(d, carry):
                body(d)
                return carry

            lax.fori_loop(first, groups, step, 0)

    order = [(i, lax.rem(z + i + 1, zs)) for i in range(zs)]

    barrier = pltpu.get_barrier_semaphore()
    for i, q in order:
        def greet(d, q=q):
            pl.semaphore_signal(
                barrier, inc=1, device_id=(lax.rem(me + d, groups), q * PAIR + y), device_id_type=MESH
            )

        for_groups(1 if i == zs - 1 else 0, greet)
    pl.semaphore_signal(barrier, inc=1, device_id=(me, other), device_id_type=MESH)

    def piece(ref, p):
        if ref.shape[0] == 1:
            return ref.at[0, :, pl.ds(pl.multiple_of(p * width, width), width)]
        return ref.at[p]

    loads = [
        pltpu.make_async_copy(piece(tokens_ref, me), inbox.at[me, 0], w_sems.at[3]),
        pltpu.make_async_copy(piece(cotangent_ref, me), inbox.at[me, 1], w_sems.at[4]),
        pltpu.make_async_copy(gate_up_ref.at[0], weights.at[:, pl.ds(0, slc)], w_sems.at[0]),
        pltpu.make_async_copy(gate_up_ref.at[1], weights.at[:, pl.ds(slc, slc)], w_sems.at[1]),
        pltpu.make_async_copy(down_ref, weights.at[:, pl.ds(2 * slc, slc)], w_sems.at[2]),
    ]
    for load in loads:
        load.start()

    lanes = metas.shape[-1]
    lane = lax.broadcasted_iota(jnp.int32, (8, lanes), 1)
    line = lax.broadcasted_iota(jnp.int32, (8, lanes), 0)

    def slots(group, row):
        return group * block + lax.rem(row, block)

    lane_row, lane_group = lax.rem(lane, tok), lax.rem(lax.div(lane, tok), groups)
    lane_block = lax.div(lane_row, block)
    lane_expert = lax.div(slots(lane_group, lane_row), cap)
    own_dest = sum(jnp.where(lane_block == b, dest_ref[0, 0, b], 0) for b in range(groups))
    own_count = sum(jnp.where(lane_expert == e, counts_ref[0, 0, e], 0) for e in range(experts))
    metas[me] = jnp.where(line == 0, own_dest, own_count)

    pl.semaphore_wait(barrier, groups * zs)

    def remote(src, dst, sems, at, device):
        return pltpu.make_async_remote_copy(
            src_ref=src, dst_ref=dst, send_sem=sems.at[0, at], recv_sem=sems.at[1, at],
            device_id=device, device_id_type=MESH,
        )

    sent = []

    meta_copies = [remote(metas.at[me], metas.at[me], meta_sems, d, (p, ep)) for d, p in grp_peers]
    pack_copies = [
        [
            remote(piece(ref, p), inbox.at[me, t], pack_sems, t * groups + d, (p, ep))
            for d, p in grp_peers
        ]
        for t, ref in enumerate((tokens_ref, cotangent_ref))
    ]
    for copy in meta_copies + pack_copies[0] + pack_copies[1]:
        copy.start()
    sent += meta_copies + pack_copies[0] + pack_copies[1]

    m = lax.broadcasted_iota(jnp.int32, (1, n_rows), 1)
    m_group, m_row = lax.rem(lax.div(m, tok), groups), lax.rem(m, tok)
    slot = slots(m_group, m_row)
    row_at = lax.broadcasted_iota(jnp.int32, (rows, tok), 0)

    for copy in meta_copies:
        copy.wait_recv()
    dest = sum(jnp.where(m_group == g, metas[g, 0:1, 0:n_rows], 0) for g in range(groups))
    kept = sum(
        jnp.where((dest == h) & (lax.rem(slot, cap) < metas[h, 1:2, 0:n_rows]), 1, 0)
        for h in range(groups)
    )
    home = jnp.where(kept > 0, dest * tok + slot, -1)

    def own_rows(t):
        loads[t].wait()
        for copy in pack_copies[t]:
            copy.wait_recv()
        picked = jnp.zeros((rows, width), F32)
        for g in range(groups):
            place = jnp.where(row_at == home[:, g * tok:(g + 1) * tok], 1.0, 0.0).astype(BF16)
            picked = picked + dot(place, inbox[g, t], (1, 0))
        xall[0, z, t] = picked.astype(BF16)

    def to_other(t, at, source):
        return remote(xall.at[0, source, t], xall.at[1, source, t], y_sems, t * zs + at, (me, other))

    def along(t, d):
        return remote(
            xall.at[0, z, t], xall.at[0, z, t], z_sems, t * zs + d, (me, lax.rem(z + d, zs) * PAIR + y)
        )

    def send_own(t):
        to_other(t, 0, z).start()
        for d in range(1, zs):
            along(t, d).start()

    def pass_on(t):
        for d in range(1, zs):
            along(t, d).wait_recv()
            to_other(t, d, lax.rem(z + zs - d, zs)).start()

    def arrivals(t):
        for d in range(zs):
            to_other(t, d, lax.rem(z + zs - d, zs)).wait_recv()

    def passed(t):
        for d in range(zs):
            if d > 0:
                along(t, d).wait_send()
            to_other(t, d, lax.rem(z + zs - d, zs)).wait_send()

    def x_rows(side, first, kind):
        return xall[side, pl.ds(first, per_dot), kind].reshape(per_dot * rows, width)

    def each(body):
        def step(i, carry):
            body(i * per_dot)
            return carry

        lax.fori_loop(0, zs // per_dot, step, 0)

    def project(side, kind, low, high, target):
        def step(first):
            out = dot(x_rows(side, first, kind), weights[:, low * slc:high * slc], (1, 0))
            target[pl.ds(side * zs + first, per_dot)] = (
                out.astype(BF16).reshape(per_dot, rows, (high - low) * slc)
            )

        each(step)

    def send_parts(t, source, target):
        copies = [
            remote(source.at[pl.ds(p * share, share)], target.at[me], part_sems, t * groups + d, (p, ep))
            for d, p in grp_peers
        ]
        for copy in copies:
            copy.start()
        return copies

    held = pl.ds(me * share, share)

    def summed(copies, source, target):
        total = source[held].astype(F32)
        for d, copy in zip(range(1, groups), copies):
            copy.wait_recv()
            total = total + target[lax.rem(me + groups - d, groups)].astype(F32)
        return total

    def share_out(t, ref):
        copies = [
            remote(ref.at[held], ref.at[held], grad_sems, t * groups + d, (p, ep))
            for d, p in grp_peers
        ]
        for copy in copies:
            copy.start()
        return copies

    def only_served(value):
        if experts == 1:
            return value
        row = lax.broadcasted_iota(jnp.int32, value.shape, 1)
        expert = lax.div(lax.rem(row, tok), cap)
        return jnp.where(expert == lax.div(placement_ref[ep], split), value, 0.0)

    def rows_of(ref, side, first):
        return ref[pl.ds(side * zs + first, per_dot)].reshape(per_dot * rows, ref.shape[-1])

    def produce(side, kind, target):
        def step(first):
            source, low, high = ((hidden, 2, 3), (grads, 0, 2))[kind]
            out = dot(rows_of(source, side, first), turned[low * slc:high * slc, :], (1, 0))
            target[pl.ds(first, per_dot), kind] = out.astype(target.dtype).reshape((per_dot,) + target.shape[2:])

        each(step)

    def send_across(t):
        copies = [
            remote(outrows.at[q, t], yin.at[q, t], yo_sems, t * zs + i, (me, other)) for i, q in order
        ]
        for copy in copies:
            copy.start()
        return copies

    def deliver(t, i, q, d):
        p = lax.rem(me + d, groups)
        return remote(
            placed.at[q, t, p], zin.at[z, me, t], zo_sems, (t * zs + i) * groups + d, (p, q * PAIR + y)
        )

    def send_home(t, copies):
        for i, q in order:
            copies[i].wait()
            total = mine[q, t].astype(F32) + yin[q, t].reshape(rows, width).astype(F32)
            for p in range(groups):
                placed[q, t, p] = total[p * tok:(p + 1) * tok].astype(BF16)

            def send(d, i=i, q=q):
                deliver(t, i, q, d).start()

            for_groups(1 if i == zs - 1 else 0, send)
            if i == zs - 1:
                zin[z, me, t] = placed[q, t, me]

    def delivered(t, wait):
        for i, q in order:
            for_groups(1 if i == zs - 1 else 0, lambda d, i=i, q=q: wait(deliver(t, i, q, d)))

    for t in range(2):
        own_rows(t)
        send_own(t)
    for load in loads[2:]:
        load.wait()
    turned[...] = jnp.transpose(weights[...], (1, 0))
    pass_on(0)
    project(0, 0, 0, 2, part_gu)
    pass_on(1)
    arrivals(0)
    project(1, 0, 0, 2, part_gu)
    gu_copies = send_parts(0, part_gu, in_gu)
    project(0, 1, 2, 3, part_h)

    gate_up = summed(gu_copies, part_gu, in_gu)
    gate, up_part = gate_up[:, :, 0:slc], gate_up[:, :, slc:2 * slc]
    sig = jax.nn.sigmoid(gate)
    activated = gate * sig
    hidden[held] = only_served(activated * up_part).astype(BF16)
    hidden_copies = share_out(0, hidden)

    arrivals(1)
    project(1, 1, 2, 3, part_h)
    h_copies = send_parts(1, part_h, in_h)

    for copy in hidden_copies:
        copy.wait_recv()
    produce(1, 0, outrows)
    across_ahead = send_across(0)
    produce(0, 0, mine)

    hidden_grad = summed(h_copies, part_h, in_h)
    gate_grad = hidden_grad * up_part * sig * (1.0 + gate * (1.0 - sig))
    grads[held, :, 0:slc] = only_served(gate_grad).astype(BF16)
    grads[held, :, slc:2 * slc] = only_served(hidden_grad * activated).astype(BF16)
    grad_copies = share_out(1, grads)

    send_home(0, across_ahead)

    for copy in grad_copies:
        copy.wait_recv()
    produce(1, 1, outrows)
    across_back = send_across(1)
    produce(0, 1, mine)

    def weight_grad(kind, ref, low, high):
        at = slice(low * slc, high * slc)
        if blocks == PAIR * per_dot:
            acc[:, at] = dot(
                xall[:, :, kind].reshape(blocks * rows, width),
                ref[...].reshape(blocks * rows, ref.shape[-1]), (0, 0),
            )
            return
        acc[:, at] = jnp.zeros((width, (high - low) * slc), F32)
        for side in range(PAIR):
            def step(first, side=side):
                acc[:, at] += dot(x_rows(side, first, kind), rows_of(ref, side, first), (0, 0))

            each(step)

    weight_grad(1, hidden, 2, 3)
    down_held[...] = acc[:, 2 * slc:3 * slc].astype(down_held.dtype)
    stores = [
        pltpu.make_async_copy(down_held, down_out, o_sems.at[0]),
        pltpu.make_async_copy(gate_up_held, gate_up_out, o_sems.at[1]),
    ]
    stores[0].start()
    send_home(1, across_back)
    weight_grad(0, grads, 0, 2)
    for i in range(2):
        gate_up_held[i] = acc[:, i * slc:(i + 1) * slc].astype(gate_up_held.dtype)
    stores[1].start()

    for t in range(2):
        delivered(t, lambda copy: copy.wait_recv())
        for g in range(groups):
            total = zin[0, g, t].astype(F32)
            for q in range(1, zs):
                total = total + zin[q, g, t].astype(F32)
            total = total.astype(BF16)
            if rows_out.shape[0] == 2:
                rows_out[t, :, g * width:(g + 1) * width] = total
            else:
                rows_out[g, t] = total
    sent += gu_copies + h_copies + hidden_copies + grad_copies
    for store in stores:
        store.wait()
    for copy in sent:
        copy.wait_send()
    for t in range(2):
        passed(t)
        delivered(t, lambda copy: copy.wait_send())


def body(tokens, cotangent, counts, destination, placement, gate_up_weight, down_weight):
    groups = lax.axis_size("grp")
    owners = lax.axis_size("ep")
    tok, model = tokens.shape[1], tokens.shape[2]
    experts = counts.shape[2]
    split = owners // experts
    width, slc = down_weight.shape[1], down_weight.shape[2]
    zs = owners // PAIR
    rows = groups * tok
    per_dot = min(zs, max(1, 64 // rows))
    lanes = -(-2 * rows // 128) * 128
    if width % 128:
        tokens, cotangent = (
            jnp.transpose(v[0].reshape(tok, groups, width), (1, 0, 2)) for v in (tokens, cotangent)
        )

    blocks = PAIR * zs
    share = blocks // groups
    vmem = pl.BlockSpec(memory_space=pltpu.VMEM)
    smem = pl.BlockSpec(memory_space=pltpu.SMEM)
    hbm = pl.BlockSpec(memory_space=pltpu.HBM)
    large = zs * rows * width >= (1 << 20)
    flat = (groups, tok, width) if large else (rows, width)
    shapes = [
        ((groups, 2, tok, width), BF16),
        ((groups, 8, lanes), jnp.int32),
        ((PAIR, zs, 2, rows, width), BF16),
        ((width, 3 * slc), BF16),
        ((3 * slc, width), BF16),
        ((blocks, rows, 2 * slc), BF16),
        ((blocks, rows, slc), BF16),
        ((groups, share, rows, 2 * slc), BF16),
        ((groups, share, rows, slc), BF16),
        ((blocks, rows, slc), BF16),
        ((blocks, rows, 2 * slc), BF16),
        ((zs, 2) + flat, BF16),
        ((zs, 2, rows, width), BF16 if large else F32),
        ((zs, 2) + flat, BF16),
        ((1, 1, 1, tok, width) if large else (zs, 2, groups, tok, width), BF16),
        ((zs, groups, 2, tok, width), BF16),
        ((width, 3 * slc), F32),
        ((2, width, slc), BF16),
        ((width, slc), BF16),
    ]
    dma = pltpu.SemaphoreType.DMA
    out, gate_up_grad, down_grad = pl.pallas_call(
        functools.partial(kernel, (groups, zs, tok, experts, split, per_dot)),
        out_shape=(
            jax.ShapeDtypeStruct((groups, 2, tok, width) if width % 128 else (2, tok, model), BF16),
            jax.ShapeDtypeStruct((2, width, slc), BF16),
            jax.ShapeDtypeStruct((width, slc), BF16),
        ),
        in_specs=[hbm, hbm, smem, smem, smem, hbm, hbm],
        out_specs=(vmem, hbm, hbm),
        scratch_shapes=[pltpu.VMEM(s, t) for s, t in shapes] + [
            dma((2, 2 * groups)), dma((2, groups)), dma((2, 2 * zs)), dma((2, 2 * zs)),
            dma((2, 2 * groups)), dma((2, 2 * groups)), dma((2, 2 * zs)), dma((2, 2 * zs * groups)), dma((5,)), dma((2,)),
        ],
        compiler_params=pltpu.CompilerParams(
            collective_id=0, has_side_effects=True, vmem_limit_bytes=60 << 20
        ),
    )(tokens, cotangent, destination, counts, placement, gate_up_weight[0], down_weight[0])
    if width % 128:
        out = jnp.transpose(out, (1, 2, 0, 3)).reshape(2, tok, model)
    return out[0:1], out[1:2], gate_up_grad[None].astype(F32), down_grad[None].astype(F32)


def solution(mesh):
    return jax.shard_map(
        body,
        mesh=mesh,
        in_specs=(
            P("grp", "ep", None),
            P("grp", "ep", None),
            P("grp", "ep", None),
            P("grp", "ep", None),
            P(),
            P("ep", None, "grp", None),
            P("ep", "grp", None),
        ),
        out_specs=(
            P("grp", "ep", None),
            P("grp", "ep", None),
            P("ep", None, "grp", None),
            P("ep", "grp", None),
        ),
        check_vma=False,
    )
```
